128 devices in a mesh: row: 16 (over x, y), col: 8 (over z, core).
Axes of the slice: x: 4, y: 4, z: 4, core: 2. Of those that a mesh axis runs over, the one named last changes fastest.
Arguments:
- pair_rep: bfloat16 [512, 512, 128], P(('row', 'col')), may hold values from -16 to 16
- tile_mask: int32 [4, 4], replicated, may hold values from 0 to 1, as said below
- chain_ids: int32 [512], replicated, may hold values from 0 to 3, never falling along the last dimension, each value on 1 to 256 neighbouring positions
- chain_bias: float32 [2, 4], replicated, may hold values from -6 to 6
- row_project: bfloat16 [128, 512], replicated, may hold values from -0.5 to 0.5
- row_bias_proj: bfloat16 [128, 4], replicated, may hold values from -36 to 36
- row_output: bfloat16 [128, 128], replicated, may hold values from -0.5 to 0.5
- col_project: bfloat16 [128, 512], replicated, may hold values from -0.5 to 0.5
- col_bias_proj: bfloat16 [128, 4], replicated, may hold values from -36 to 36
- col_output: bfloat16 [128, 128], replicated, may hold values from -0.5 to 0.5
- tri_left: bfloat16 [128, 256], replicated, may hold values from -0.5 to 0.5
- tri_right: bfloat16 [128, 256], replicated, may hold values from -0.5 to 0.5
- tri_gate: bfloat16 [128, 128], replicated, may hold values from -0.5 to 0.5
- tri_output: bfloat16 [128, 128], replicated, may hold values from -1.5 to 1.5
Outputs:
- pair_out: bfloat16 [512, 512, 128], P('row', 'col')
The draws below stay inside these ranges and needn't reach their ends.
Inputs may be any that keep to these rules, and one draw needn't show every extreme that they name: `tile_mask`: every diagonal entry is 1. `chain_ids`: chain numbers never fall along the residues.
All inputs are finite; a program needn't handle non-finite values.
Results may differ from the reference program's by a relative error of at most 0.018.
Values may be sent and summed in bfloat16 or wider, within the bound.
A program may use at most 64 MiB of HBM per device.

```python
import math
import jax
import jax.numpy as jnp
import numpy as np
from jax import lax

C = 128
HEADS = 4
HEAD_DIM = 32
TILE = 128
CHAINS = 4
RES = 512
TILES = 4


def bias_weights(key):
    row_part = jax.random.truncated_normal(jax.random.fold_in(key, 17), -3.0, 3.0, (C, HEADS), jnp.float32) * (0.75 * C ** (-0.5))
    col_part = jax.random.truncated_normal(jax.random.fold_in(key, 29), -3.0, 3.0, (C, HEADS), jnp.float32) * (0.75 * C ** (-0.5))
    return (row_part, col_part)


def draw_row_bias_proj(key, part):
    return bias_weights(key)[0].astype(jnp.bfloat16)


def draw_col_bias_proj(key, part):
    return bias_weights(key)[1].astype(jnp.bfloat16)


def draw_pair_rep(key, part):
    values = jax.random.truncated_normal(jax.random.fold_in(key, 3), -4.0, 4.0, (RES, RES, C), jnp.float32)
    return values.astype(jnp.bfloat16)


def draw_tile_mask(key, part):
    density = jax.random.randint(jax.random.fold_in(key, 41), (TILES, 1), 0, 2)
    rolled = jax.random.randint(jax.random.fold_in(key, 43), (TILES, TILES), 0, 8)
    diagonal = jnp.arange(TILES)[:, None] == jnp.arange(TILES)[None, :]
    return jnp.where(diagonal, 1, (rolled < density).astype(jnp.int32)).astype(jnp.int32)


def length_profile(number_of, total, bound, skew):
    portions = [(1 << 20) // math.isqrt(standing ** skew) + 1 for standing in range(2, number_of + 1)]
    rest, given = total - bound - (number_of - 1), [1] * (number_of - 1)
    while rest > 0:
        free = [i for i in range(number_of - 1) if given[i] < bound]
        pool, budget = sum([portions[i] for i in free]), rest
        for i in free:
            extra = min(bound - given[i], max(1, budget * portions[i] // pool), rest)
            given[i] = given[i] + extra
            rest = rest - extra
    return np.array([bound] + given)


def uneven(key, number_of, total, bound, lean):
    if number_of == 2:
        one = jax.random.randint(key, (), max(1, total - bound), min(bound, total - 1) + 1)
        return jnp.stack([one, total - one])
    lengths = jnp.asarray(length_profile(number_of, total, bound, lean), jnp.int32)
    twos = (number_of - 1) // 2
    giver, receiver = lengths[1:1 + 2 * twos:2], lengths[2:2 + 2 * twos:2]
    slack = jnp.minimum(giver - 1, bound - receiver)
    shifted = jax.random.randint(jax.random.fold_in(key, 1), (twos,), 0, 1 << 20) % (slack + 1)
    lengths = lengths.at[1:1 + 2 * twos:2].set(giver - shifted).at[2:2 + 2 * twos:2].set(receiver + shifted)
    return lengths[jax.random.permutation(jax.random.fold_in(key, 2), number_of)]


def bell_draw(rng, shape, scale, reach, dtype=jnp.bfloat16):
    result = scale * jax.random.normal(rng, shape, jnp.float32)
    return jnp.clip(result, min=-reach, max=reach).astype(dtype)


def setup_inputs(seed: int = 0) -> dict:
    seeds = jax.random.split(jax.random.key(seed), 15)
    pair_rep = draw_pair_rep(jax.random.fold_in(seeds[14], 71), 0)
    tile_mask = draw_tile_mask(jax.random.fold_in(seeds[14], 71), 0)
    chain_ids = jnp.searchsorted(jnp.cumsum(uneven(seeds[2], CHAINS, RES, RES // 2, 1)), jnp.arange(RES), side="right").astype(jnp.int32)
    chain_bias = bell_draw(seeds[3], (2, HEADS), 1.5, 6.0, jnp.float32)
    row_project = bell_draw(seeds[4], (C, 4 * C), C ** -0.5, 0.5)
    row_bias_proj = draw_row_bias_proj(jax.random.fold_in(seeds[14], 71), 0)
    row_output = bell_draw(seeds[6], (C, C), C ** -0.5, 0.5)
    col_project = bell_draw(seeds[7], (C, 4 * C), C ** -0.5, 0.5)
    col_bias_proj = draw_col_bias_proj(jax.random.fold_in(seeds[14], 71), 0)
    col_output = bell_draw(seeds[9], (C, C), C ** -0.5, 0.5)
    tri_left = bell_draw(seeds[10], (C, 2 * C), C ** -0.5, 0.5)
    tri_right = bell_draw(seeds[11], (C, 2 * C), C ** -0.5, 0.5)
    tri_gate = bell_draw(seeds[12], (C, C), C ** -0.5, 0.5)
    tri_output = bell_draw(seeds[13], (C, C), (C / 9) ** -0.5, 1.5)
    return {"pair_rep": pair_rep, "tile_mask": tile_mask, "chain_ids": chain_ids, "chain_bias": chain_bias, "row_project": row_project, "row_bias_proj": row_bias_proj, "row_output": row_output, "col_project": col_project, "col_bias_proj": col_bias_proj, "col_output": col_output, "tri_left": tri_left, "tri_right": tri_right, "tri_gate": tri_gate, "tri_output": tri_output}


def layer_norm(values):
    values = values.astype(jnp.float32)
    center = values - lax.optimization_barrier(jnp.mean(values, axis=-1, keepdims=True))
    spread = lax.optimization_barrier(jnp.mean(center * center, axis=-1, keepdims=True))
    return center * lax.rsqrt(spread + 1e-05)

def triangle_attention(pair_in, allowed, chain_ids, chain_add, project, bias_proj, output):
    normed = layer_norm(pair_in).astype(jnp.bfloat16)
    flat_rows = normed.reshape(RES * RES, C)
    projected = jnp.dot(flat_rows, project, preferred_element_type=jnp.float32).reshape(RES, RES, 4 * C)
    queries = projected[..., :C].astype(jnp.bfloat16).reshape(RES, RES, HEADS, HEAD_DIM)
    key_rows = projected[..., C:2 * C].astype(jnp.bfloat16).reshape(RES, RES, HEADS, HEAD_DIM)
    value_rows = projected[..., 2 * C:3 * C].astype(jnp.bfloat16).reshape(RES, RES, HEADS, HEAD_DIM)
    bias_all = jnp.dot(flat_rows, bias_proj, preferred_element_type=jnp.float32).reshape(RES, RES, HEADS).transpose(2, 0, 1)
    same_chain = (chain_ids[:, None] == chain_ids[None, :]).astype(jnp.float32)

    def one_line(inputs):
        query_line, key_line, value_line, usable = inputs
        scores = jnp.einsum('qhd,khd->hqk', query_line.astype(jnp.float32), key_line.astype(jnp.float32)) * HEAD_DIM ** (-0.5)
        scores = scores + bias_all
        scores = scores + chain_add[:, None, None] * same_chain[None]
        scores = jnp.where(usable[None, None, :], scores, -1000000000.0)
        row_peak = lax.optimization_barrier(jnp.max(scores, axis=-1, keepdims=True))
        weights = jnp.exp(scores - row_peak)
        attention = (weights / lax.optimization_barrier(jnp.sum(weights, axis=-1, keepdims=True))).astype(jnp.bfloat16)
        mixed_rows = jnp.einsum('hqk,khd->qhd', attention.astype(jnp.float32), value_line.astype(jnp.float32))
        return mixed_rows.reshape(RES, C)
    mixed_all = lax.map(one_line, (queries, key_rows, value_rows, allowed))
    gated = (mixed_all * jax.nn.sigmoid(projected[..., 3 * C:])).astype(jnp.bfloat16)
    update = jnp.dot(gated.reshape(RES * RES, C), output, preferred_element_type=jnp.float32).reshape(RES, RES, C)
    return (pair_in.astype(jnp.float32) + update).astype(jnp.bfloat16)

def reference(pair_rep, tile_mask, chain_ids, chain_bias, row_project, row_bias_proj, row_output, col_project, col_bias_proj, col_output, tri_left, tri_right, tri_gate, tri_output):
    allowed = jnp.repeat(jnp.repeat(tile_mask, TILE, axis=0), TILE, axis=1) > 0
    first_pair = triangle_attention(pair_rep, allowed, chain_ids, chain_bias[0], row_project, row_bias_proj, row_output)
    flipped = triangle_attention(first_pair.transpose(1, 0, 2), allowed.T, chain_ids, chain_bias[1], col_project, col_bias_proj, col_output)
    second_pair = flipped.transpose(1, 0, 2)
    normed = layer_norm(second_pair).astype(jnp.bfloat16)
    flat_rows = normed.reshape(RES * RES, C)
    mask_float = allowed.astype(jnp.float32)
    left_proj = jnp.dot(flat_rows, tri_left, preferred_element_type=jnp.float32).reshape(RES, RES, 2 * C)
    right_proj = jnp.dot(flat_rows, tri_right, preferred_element_type=jnp.float32).reshape(RES, RES, 2 * C)
    left_act = (jax.nn.sigmoid(left_proj[..., C:]) * left_proj[..., :C] * mask_float[..., None]).astype(jnp.bfloat16)
    right_act = (jax.nn.sigmoid(right_proj[..., C:]) * right_proj[..., :C] * mask_float[..., None]).astype(jnp.bfloat16)
    product_sum = jnp.einsum('ikc,jkc->ijc', left_act.astype(jnp.float32), right_act.astype(jnp.float32))
    centered = layer_norm(product_sum).astype(jnp.bfloat16)
    gate_values = jax.nn.sigmoid(jnp.dot(flat_rows, tri_gate, preferred_element_type=jnp.float32).reshape(RES, RES, C))
    update = jnp.dot(centered.reshape(RES * RES, C), tri_output, preferred_element_type=jnp.float32).reshape(RES, RES, C)
    return (second_pair.astype(jnp.float32) + gate_values * update).astype(jnp.bfloat16)
```

```python
import functools
import math

import jax
import jax.numpy as jnp
from jax import lax
from jax.experimental import pallas as pl
from jax.experimental.pallas import tpu as pltpu
from jax.sharding import PartitionSpec as P

MESH = pl.DeviceIdType.MESH
F32 = jnp.float32
BF16 = jnp.bfloat16
DEVS = 128
LOG2E = 1.4426950408889634
VMEM_LIMIT = 50 * 2**20


def vmem():
    return pl.BlockSpec(memory_space=pltpu.VMEM)


def smem():
    return pl.BlockSpec(memory_space=pltpu.SMEM)


def layer_norm(values):
    center = values - jnp.mean(values, axis=-1, keepdims=True)
    spread = jnp.mean(center * center, axis=-1, keepdims=True)
    return center * lax.rsqrt(spread + 1e-05)


def dot(a, b, ca=1, cb=0):
    return lax.dot_general(a, b, (((ca,), (cb,)), ((), ())), preferred_element_type=F32)


def sigmoid(x):
    return 1.0 / (1.0 + jnp.exp(-x))


def my_place():
    row, col = lax.axis_index("row"), lax.axis_index("col")
    return row, col, row * 8 + col


def drain(ref, sem):
    pltpu.make_async_copy(ref, ref, sem).wait()


def write_bias_block(blk_ref, line, bias):
    for half in range(2):
        for tile in range(4):
            blk_ref[half, tile, 2 * line : 2 * line + 2, :] = bias[
                2 * half : 2 * half + 2, tile * 128 : (tile + 1) * 128
            ]


def greet(partners):
    barrier = pltpu.get_barrier_semaphore()
    for partner in partners:
        pl.semaphore_signal(barrier, inc=1, device_id=partner, device_id_type=MESH)
    pl.semaphore_wait(barrier, len(partners))


def gather_partners():
    row, col, _ = my_place()
    core, z, y, x = col % 2, col // 2, row % 4, row // 4
    sibling = (row, z * 2 + 1 - core)
    partners = [sibling]
    for step in (1, 2, 3):
        partners.append((row, (z + step) % 4 * 2 + core))
        partners.append((x * 4 + (y + step) % 4, col))
        partners.append(((x + step) % 4 * 4 + y, col))
    return partners


def gather_bias(blk_ref, g_ref, own_sem, zs, zr, as_, ar_, bs, br, fs, fr):
    row, col, dev = my_place()
    core, z, y, x = col % 2, col // 2, row % 4, row // 4
    a_me = jnp.where(core == 0, y, x)
    b_me = jnp.where(core == 0, x, y)
    sibling = (row, z * 2 + 1 - core)

    def row_of(a, b):
        a, b = lax.rem(a, 4), lax.rem(b, 4)
        return jnp.where(core == 0, b * 4 + a, a * 4 + b)

    def part(half, start, size):
        return g_ref.at[half, :, pl.ds(pl.multiple_of(start, 8), size), :]

    started = []

    def send(src, dst, ssem, rsem, device):
        copy = pltpu.make_async_remote_copy(
            src_ref=src, dst_ref=dst, send_sem=ssem, recv_sem=rsem, device_id=device, device_id_type=MESH
        )
        copy.start()
        started.append(copy)

    def arrived(ref, sem):
        drain(ref, sem)

    own = pltpu.make_async_copy(blk_ref.at[core], part(core, dev * 8, 8), own_sem.at[0])
    own.start()
    send(blk_ref.at[1 - core], part(1 - core, dev * 8, 8), own_sem.at[1], own_sem.at[2], sibling)
    own.wait()
    sib_dev = row * 8 + z * 2 + 1 - core
    arrived(part(core, sib_dev * 8, 8), own_sem.at[2])

    chip = part(core, (row * 8 + z * 2) * 8, 16)
    for step in (1, 3, 2):
        send(chip, chip, zs.at[step], zr.at[4 - step], (row, lax.rem(z + step, 4) * 2 + core))
    for step in (1, 3, 2):
        arrived(part(core, (row * 8 + lax.rem(z + step, 4) * 2) * 8, 16), zr.at[step])

    def block(da, db):
        return part(core, row_of(a_me + da, b_me + db) * 64, 64)

    def to_sibling(da, db):
        ref = block(da, db)
        send(ref, ref, fs.at[da * 4 + db], fr.at[da * 4 + db], sibling)

    def along_b(da, db, step):
        ref = block(da, db)
        rel = (db - step) % 4
        send(ref, ref, bs.at[da * 4 + rel], br.at[da * 4 + rel], (row_of(a_me, b_me + step), col))

    for step in (1, 3, 2):
        ref = block(0, 0)
        send(ref, ref, as_.at[step], ar_.at[4 - step], (row_of(a_me + step, b_me), col))
    along_b(0, 0, 1)
    along_b(0, 0, 3)
    to_sibling(0, 0)
    for da in (1, 3, 2):
        arrived(block(da, 0), ar_.at[da])
        along_b(da, 0, 1)
        along_b(da, 0, 3)
        to_sibling(da, 0)
    for da in (0, 1, 3, 2):
        arrived(block(da, 3), br.at[da * 4 + 3])
        if da in (0, 3):
            along_b(da, 3, 1)
        to_sibling(da, 3)
        arrived(block(da, 1), br.at[da * 4 + 1])
        if da in (1, 2):
            along_b(da, 1, 3)
        to_sibling(da, 1)
    for da in (0, 1, 3, 2):
        arrived(block(da, 2), br.at[da * 4 + 2])
        to_sibling(da, 2)

    def finish():
        for da in range(4):
            for db in range(4):
                s_row = jnp.where(
                    core == 1,
                    lax.rem(x + db, 4) * 4 + lax.rem(y + da, 4),
                    lax.rem(x + da, 4) * 4 + lax.rem(y + db, 4),
                )
                arrived(part(1 - core, s_row * 64, 64), fr.at[da * 4 + db])
        for copy in started:
            copy.wait_send()

    return finish


GATHER_SEMS = [pltpu.SemaphoreType.DMA((n,)) for n in (3, 4, 4, 4, 4, 16, 16, 16, 16)]
G_SHAPE = (2, 4, 1024, 128)


def start_kernel(x_ref, bias_w_ref, g_ref, blk, *sems):
    for line in range(4):
        normed = layer_norm(x_ref[line].astype(F32)).astype(BF16)
        write_bias_block(blk, line, dot(bias_w_ref[...], normed, 0, 1))
    greet(gather_partners())
    gather_bias(blk, g_ref, *sems)()


def start(x, bias_w):
    return pl.pallas_call(
        start_kernel,
        out_shape=jax.ShapeDtypeStruct(G_SHAPE, F32),
        in_specs=[vmem(), vmem()],
        out_specs=vmem(),
        scratch_shapes=[pltpu.VMEM((2, 4, 8, 128), F32)] + GATHER_SEMS,
        compiler_params=pltpu.CompilerParams(
            collective_id=0, has_side_effects=True, vmem_limit_bytes=VMEM_LIMIT
        ),
        name="bias_gather",
    )(x, bias_w)


def all_to_all_start(src_ref, dst_ref, ssem, rsem, lsem):
    row, col, dev = my_place()
    pltpu.make_async_copy(src_ref.at[dev], dst_ref.at[dev], lsem).start()

    def step(off, carry):
        dest = lax.rem(dev + off, DEVS)
        pltpu.make_async_remote_copy(
            src_ref=src_ref.at[dest],
            dst_ref=dst_ref.at[dev],
            send_sem=ssem,
            recv_sem=rsem,
            device_id=(dest // 8, dest % 8),
            device_id_type=MESH,
        ).start()
        return carry

    lax.fori_loop(1, DEVS, step, 0)


def all_to_all_recv(src_ref, dst_ref, ssem, rsem, lsem):
    rest = dst_ref.at[pl.ds(0, DEVS - 1)]
    drain(dst_ref.at[0], lsem)
    drain(rest, rsem)


def all_to_all_sent(src_ref, dst_ref, ssem, rsem, lsem):
    drain(src_ref.at[pl.ds(0, DEVS - 1)], ssem)


def greet_all():
    _, _, dev = my_place()
    barrier = pltpu.get_barrier_semaphore()

    def step(off, carry):
        dest = lax.rem(dev + off, DEVS)
        pl.semaphore_signal(barrier, inc=1, device_id=(dest // 8, dest % 8), device_id_type=MESH)
        return carry

    lax.fori_loop(1, DEVS, step, 0)
    pl.semaphore_wait(barrier, DEVS - 1)


def middle_kernel(blk_ref, pair_ref, g_ref, cols_ref, s0, s1, s2, *sems):
    greet_all()
    args = (pair_ref, cols_ref, s0, s1, s2)
    all_to_all_start(*args)
    finish = gather_bias(blk_ref, g_ref, *sems)
    finish()
    all_to_all_recv(*args)
    all_to_all_sent(*args)


def middle(blk, pair):
    return pl.pallas_call(
        middle_kernel,
        out_shape=(jax.ShapeDtypeStruct(G_SHAPE, F32), jax.ShapeDtypeStruct((128, 16, 128), BF16)),
        in_specs=[vmem(), vmem()],
        out_specs=(vmem(), vmem()),
        scratch_shapes=[pltpu.SemaphoreType.DMA] * 3 + GATHER_SEMS,
        compiler_params=pltpu.CompilerParams(
            collective_id=1, has_side_effects=True, vmem_limit_bytes=VMEM_LIMIT
        ),
        name="columns_and_bias",
    )(blk, pair)


def compact(flags):
    count = jnp.int32(0)
    picked = [jnp.int32(0)] * 4
    for tile in range(4):
        for place in range(4):
            hit = jnp.logical_and(flags[tile] > 0, count == place)
            picked[place] = jnp.where(hit, tile, picked[place])
        count = count + flags[tile]
    return picked, count


def attention(
    first, lines, flags, g_ref, ids_ref, chain_add, project_ref, output_ref, emit, k_buf, q_buf, v_buf, gate_buf, mix_buf, ids_buf
):
    scale = LOG2E * 32 ** (-0.5)
    w_k = project_ref[:, 128:256]
    w_q = project_ref[:, 0:128]
    w_vg = project_ref[:, 256:512]
    for line in range(4):
        normed = layer_norm(lines(line)).astype(BF16)
        k_buf[line] = dot(normed, w_k).astype(BF16)
        q_buf[line] = dot(w_q, normed, 0, 1).astype(BF16)
        vg = dot(w_vg, normed, 0, 1)
        v_buf[line] = vg[:128].astype(BF16)
        gate_buf[line] = sigmoid(vg[128:])
    ids = ids_ref[...].astype(F32)
    for tile in range(4):
        ids_buf[tile] = jnp.broadcast_to(ids[:, tile * 128 : (tile + 1) * 128], (128, 128)).T
    picked, count = compact(flags)

    def run(tiles):
        def body(step, carry):
            head, block = step // 2, step % 2
            half, sub = head // 2, head % 2
            q_at = pl.ds(pl.multiple_of(block * 256, 256), 256)
            head_at = pl.ds(pl.multiple_of(head * 32, 32), 32)
            head_mask = jnp.where(lax.broadcasted_iota(jnp.int32, (1, 128), 1) // 32 == head, 1.0, 0.0).astype(BF16)
            add = chain_add(head)
            q_ids = jnp.concatenate([ids_ref[:, pl.ds(pl.multiple_of(block * 256 + 128 * i, 128), 128)] for i in range(2)], axis=1)
            q_ids = q_ids.astype(F32)
            biases = []
            for place in range(tiles):
                tile = picked[place]
                if first:
                    got = g_ref[half, tile, pl.ds(block * 512 + sub, 256, stride=2), :].T
                else:
                    rows = pl.ds(tile * 256 + sub, 128, stride=2)
                    got = jnp.concatenate([g_ref[half, block * 2, rows, :], g_ref[half, block * 2 + 1, rows, :]], axis=1)
                k_ids = ids_buf[tile]
                same = jnp.concatenate([k_ids, k_ids], axis=1) == q_ids
                biases.append((got + jnp.where(same, add, 0.0)) * LOG2E)
            for line in range(4):
                q = q_buf[line, :, q_at]
                scores = []
                for place in range(tiles):
                    k_at = pl.ds(pl.multiple_of(picked[place] * 128, 128), 128)
                    keys = k_buf[line, k_at, :] * head_mask
                    scores.append(dot(keys, q) * scale + biases[place])
                peak = functools.reduce(jnp.maximum, [jnp.max(s, axis=0, keepdims=True) for s in scores])
                weights = [jnp.exp2(s - peak) for s in scores]
                total = functools.reduce(jnp.add, [jnp.sum(w, axis=0, keepdims=True) for w in weights])
                mixed = None
                for place in range(tiles):
                    k_at = pl.ds(pl.multiple_of(picked[place] * 128, 128), 128)
                    term = dot(v_buf[line, head_at, k_at], weights[place].astype(BF16))
                    mixed = term if mixed is None else mixed + term
                gated = mixed * (1.0 / total) * gate_buf[line, head_at, q_at]
                mix_buf[line, head_at, q_at] = gated.astype(BF16)
            return carry

        lax.fori_loop(0, 8, body, 0)

    for tiles in range(1, 5):
        pl.when(count == tiles)(functools.partial(run, tiles))

    w_o = output_ref[...]
    for line in range(4):
        emit(line, lines(line) + dot(mix_buf[line], w_o, 0, 0))


ATTENTION_SCRATCH = [
    pltpu.VMEM((4, 512, 128), BF16),
    pltpu.VMEM((4, 128, 512), BF16),
    pltpu.VMEM((4, 128, 512), BF16),
    pltpu.VMEM((4, 128, 512), F32),
    pltpu.VMEM((4, 128, 512), BF16),
    pltpu.VMEM((4, 128, 128), F32),
]


def row_kernel(
    mask_ref, add_ref, x_ref, g_ref, ids_ref, project_ref, output_ref, bias_w_ref, pair_ref, blk_ref, line_buf, send_buf, *scratch
):
    row, _, _ = my_place()
    flags = [mask_ref[row // 4, tile] for tile in range(4)]

    def lines(line):
        return x_ref[line].astype(F32)

    def emit(line, value):
        value = value.astype(BF16).astype(F32)
        write_bias_block(blk_ref, line, dot(bias_w_ref[...], layer_norm(value).astype(BF16), 0, 1))
        line_buf[...] = value
        for j in range(4):
            send_buf[pl.ds(line * 4 + j, 128, stride=16), :] = line_buf[pl.ds(j, 128, stride=4), :]

    attention(
        True, lines, flags, g_ref, ids_ref, lambda head: add_ref[0, head], project_ref, output_ref, emit, *scratch
    )
    pair_ref[...] = send_buf[...].reshape(128, 16, 128).astype(BF16)


def row_attention(mask, add, x, g, ids, project, output, bias_w):
    return pl.pallas_call(
        row_kernel,
        out_shape=(jax.ShapeDtypeStruct((128, 16, 128), BF16), jax.ShapeDtypeStruct((2, 4, 8, 128), F32)),
        in_specs=[smem(), smem()] + [vmem()] * 6,
        out_specs=(vmem(), vmem()),
        scratch_shapes=[pltpu.VMEM((512, 128), F32), pltpu.VMEM((2048, 128), F32)] + ATTENTION_SCRATCH,
        compiler_params=pltpu.CompilerParams(vmem_limit_bytes=VMEM_LIMIT),
        name="row_attention",
    )(mask, add, x, g, ids, project, output, bias_w)


def col_kernel(
    mask_ref,
    add_ref,
    cols_ref,
    g_ref,
    ids_ref,
    project_ref,
    output_ref,
    left_ref,
    right_ref,
    edge_ref,
    second_ref,
    cols_buf,
    edge_buf,
    *scratch,
):
    row, _, _ = my_place()
    flags = [mask_ref[tile, row // 4] for tile in range(4)]
    cols_buf[...] = cols_ref[...].astype(F32).reshape(2048, 128)

    def lines(line):
        return cols_buf[pl.ds(line, 512, stride=4), :]

    def emit(line, value):
        rounded = value.astype(BF16)
        second_ref[:, line * 32 : (line + 1) * 32, :] = rounded.reshape(16, 32, 128)
        normed = layer_norm(rounded.astype(F32)).astype(BF16)
        for side, w_ref in enumerate((left_ref, right_ref)):
            both = dot(w_ref[...], normed, 0, 1)
            act = sigmoid(both[128:]) * both[:128]
            for tile in range(4):
                edge_buf[pl.ds(line * 8 + side * 4 + tile, 128, stride=32), :] = act[
                    :, tile * 128 : (tile + 1) * 128
                ] * flags[tile].astype(F32)

    attention(
        False, lines, flags, g_ref, ids_ref, lambda head: add_ref[1, head], project_ref, output_ref, emit, *scratch
    )
    edge_ref[...] = edge_buf[...].reshape(128, 32, 128).astype(BF16)


def col_attention(mask, add, cols, g, ids, project, output, left, right):
    return pl.pallas_call(
        col_kernel,
        out_shape=(jax.ShapeDtypeStruct((128, 32, 128), BF16), jax.ShapeDtypeStruct((16, 128, 128), BF16)),
        in_specs=[smem(), smem()] + [vmem()] * 7,
        out_specs=(vmem(), vmem()),
        scratch_shapes=[pltpu.VMEM((2048, 128), F32), pltpu.VMEM((4096, 128), F32)] + ATTENTION_SCRATCH,
        compiler_params=pltpu.CompilerParams(vmem_limit_bytes=VMEM_LIMIT),
        name="col_attention",
    )(mask, add, cols, g, ids, project, output, left, right)


def triangle_kernel(
    edge_ref,
    second_ref,
    gate_w_ref,
    out_w_ref,
    out_ref,
    edge_in,
    second_in,
    edge_buf,
    prod_send,
    prod_in,
    x_buf,
    gate_buf,
    norm_buf,
    es,
    er,
    el,
    ss,
    sr,
    sl,
    ps,
    pr,
    pl_,
):
    row, col, dev = my_place()
    greet_all()
    edges = (edge_ref, edge_in, es, er, el)
    all_to_all_start(*edges)
    slot = lax.rem(dev, 16)
    grid_col = dev // 16

    def send_second(step, carry):
        to_row = lax.rem(row + step, 16)

        @pl.when(jnp.logical_and(to_row == row, grid_col == col))
        def _():
            pltpu.make_async_copy(second_ref.at[to_row], second_in.at[slot], sl).start()

        @pl.when(jnp.logical_not(jnp.logical_and(to_row == row, grid_col == col)))
        def _():
            pltpu.make_async_remote_copy(
                src_ref=second_ref.at[to_row],
                dst_ref=second_in.at[slot],
                send_sem=ss,
                recv_sem=sr,
                device_id=(to_row, grid_col),
                device_id_type=MESH,
            ).start()

        return carry

    lax.fori_loop(0, 16, send_second, 0)
    all_to_all_recv(*edges)
    edge_buf[...] = edge_in[...].astype(F32).reshape(4096, 128)
    right = jnp.concatenate([edge_buf[pl.ds(4 + tile, 512, stride=8), :] for tile in range(4)], axis=1).astype(BF16)
    low = lax.broadcasted_iota(jnp.int32, (16, 128), 1) < 64
    for tile in range(4):
        left = edge_buf[pl.ds(tile, 512, stride=8), :].astype(BF16)
        product = dot(left, right, 0, 0)
        for sub in range(4):
            for t in range(4):
                a = product[sub * 32 : sub * 32 + 16, t * 128 : (t + 1) * 128]
                b = product[sub * 32 + 16 : sub * 32 + 32, t * 128 : (t + 1) * 128]
                block = (tile * 4 + sub) * 8 + 2 * t
                prod_send[block] = jnp.where(low, a, pltpu.roll(b, 64, 1)).astype(BF16)
                prod_send[block + 1] = jnp.where(low, pltpu.roll(a, 64, 1), b).astype(BF16)
    products = (prod_send, prod_in, ps, pr, pl_)
    all_to_all_start(*products)

    own_sent = grid_col == col

    @pl.when(own_sent)
    def _():
        drain(second_in.at[0], sl)
        drain(second_in.at[pl.ds(0, 15)], sr)
        drain(second_ref.at[pl.ds(0, 15)], ss)

    @pl.when(jnp.logical_not(own_sent))
    def _():
        drain(second_in, sr)
        drain(second_ref, ss)

    gate_w = gate_w_ref[...]

    def gates(j, carry):
        at = pl.multiple_of(j * 128, 128)
        x = second_in[j].astype(F32)
        gate = sigmoid(dot(layer_norm(x).astype(BF16), gate_w))
        for sub in range(4):
            x_buf[pl.ds(j * 4 + sub, 32, stride=64), :] = x[sub * 32 : (sub + 1) * 32]
            gate_buf[pl.ds(j * 4 + sub, 32, stride=64), :] = gate[sub * 32 : (sub + 1) * 32]
        return carry

    lax.fori_loop(0, 16, gates, 0)
    all_to_all_recv(*products)
    product = prod_in[...].astype(F32)
    center = product - jnp.mean(product, axis=0, keepdims=True)
    spread = jnp.mean(center * center, axis=0, keepdims=True)
    norm_buf[...] = (center * lax.rsqrt(spread + 1e-05)).reshape(2048, 128)
    out_w = out_w_ref[...]
    for s in range(16):
        update = dot(norm_buf[pl.ds(s, 128, stride=16), :].astype(BF16), out_w, 0, 0)
        for half in range(2):
            i = half * 16 + s
            at = pl.ds(i * 64, 64)
            out_ref[i] = (x_buf[at, :] + gate_buf[at, :] * update[half * 64 : (half + 1) * 64]).astype(BF16)
    all_to_all_sent(*edges)
    all_to_all_sent(*products)


def triangle(edge, second, gate_w, out_w):
    return pl.pallas_call(
        triangle_kernel,
        out_shape=jax.ShapeDtypeStruct((32, 64, 128), BF16),
        in_specs=[vmem()] * 4,
        out_specs=vmem(),
        scratch_shapes=[
            pltpu.VMEM((128, 32, 128), BF16),
            pltpu.VMEM((16, 128, 128), BF16),
            pltpu.VMEM((4096, 128), F32),
            pltpu.VMEM((128, 16, 128), BF16),
            pltpu.VMEM((128, 16, 128), BF16),
            pltpu.VMEM((2048, 128), F32),
            pltpu.VMEM((2048, 128), F32),
            pltpu.VMEM((2048, 128), F32),
        ]
        + [pltpu.SemaphoreType.DMA] * 9,
        compiler_params=pltpu.CompilerParams(
            collective_id=2, has_side_effects=True, vmem_limit_bytes=VMEM_LIMIT
        ),
        name="triangle",
    )(edge, second, gate_w, out_w)


def shards(
    pair_rep,
    tile_mask,
    chain_ids,
    chain_bias,
    row_project,
    row_bias_proj,
    row_output,
    col_project,
    col_bias_proj,
    col_output,
    tri_left,
    tri_right,
    tri_gate,
    tri_output,
):
    ids = chain_ids.reshape(1, 512)
    g_rows = start(pair_rep, row_bias_proj)
    pair, blk = row_attention(
        tile_mask, chain_bias, pair_rep, g_rows, ids, row_project, row_output, col_bias_proj
    )
    g_cols, cols = middle(blk, pair)
    edge, second = col_attention(
        tile_mask, chain_bias, cols, g_cols, ids, col_project, col_output, tri_left, tri_right
    )
    return triangle(edge, second, tri_gate, tri_output)


def solution(mesh):
    spec = P(("row", "col"), None, None)
    return jax.shard_map(
        shards,
        mesh=mesh,
        in_specs=(spec,) + (P(),) * 13,
        out_specs=P("row", "col", None),
        check_vma=False,
    )
```

```python
import functools
import math

import jax
import jax.numpy as jnp
from jax import lax
from jax.experimental import pallas as pl
from jax.experimental.pallas import tpu as pltpu
from jax.sharding import PartitionSpec as P

MESH = pl.DeviceIdType.MESH
F32 = jnp.float32
BF16 = jnp.bfloat16
DEVS = 128
LOG2E = 1.4426950408889634
VMEM_LIMIT = 50 * 2**20


def vmem():
    return pl.BlockSpec(memory_space=pltpu.VMEM)


def smem():
    return pl.BlockSpec(memory_space=pltpu.SMEM)


def layer_norm(values):
    center = values - jnp.mean(values, axis=-1, keepdims=True)
    spread = jnp.mean(center * center, axis=-1, keepdims=True)
    return center * lax.rsqrt(spread + 1e-05)


def dot(a, b, ca=1, cb=0):
    return lax.dot_general(a, b, (((ca,), (cb,)), ((), ())), preferred_element_type=F32)


def sigmoid(x):
    return 1.0 / (1.0 + jnp.exp(-x))


def my_place():
    row, col = lax.axis_index("row"), lax.axis_index("col")
    return row, col, row * 8 + col


def drain(ref, sem):
    pltpu.make_async_copy(ref, ref, sem).wait()


def bias_step(w_ref):
    w = w_ref[...].astype(F32)
    length = jnp.sqrt(jnp.sum(w * w, axis=1, keepdims=True))
    return jnp.maximum(length, 1e-20) * (11.4 / 32766.0)


def code_bias(blk32, line, w_ref, inverse, normed):
    coded = jnp.round(dot(w_ref[...], normed, 1, 1) * inverse).astype(jnp.int32)
    for tile in range(4):
        blk32[tile // 2, tile % 2, line * 4 : line * 4 + 4, :] = coded[:, tile * 128 : (tile + 1) * 128]


def signal_partners():
    row, col, _ = my_place()
    core, z, y, x = col % 2, col // 2, row % 4, row // 4
    partners = []
    for step in range(4):
        for flip in range(2):
            if step or flip:
                partners.append((row, lax.rem(z + step, 4) * 2 + lax.rem(core + flip, 2)))
    for step in (1, 2, 3):
        partners.append((x * 4 + lax.rem(y + step, 4), col))
        partners.append((lax.rem(x + step, 4) * 4 + y, col))
    barrier = pltpu.get_barrier_semaphore()
    for partner in partners:
        pl.semaphore_signal(barrier, inc=1, device_id=partner, device_id_type=MESH)
    return len(partners)


def signal_all():
    _, _, dev = my_place()
    barrier = pltpu.get_barrier_semaphore()

    def step(off, carry):
        dest = lax.rem(dev + off, DEVS)
        pl.semaphore_signal(barrier, inc=1, device_id=(dest // 8, dest % 8), device_id_type=MESH)
        return carry

    lax.fori_loop(1, DEVS, step, 0)
    return DEVS - 1


def await_signals(count):
    pl.semaphore_wait(pltpu.get_barrier_semaphore(), count)


G_SHAPE = (2, 128, 2, 16, 128)
GATHER_SEMS = [pltpu.SemaphoreType.DMA((n,)) for n in (1, 8, 8, 4, 4, 16, 16, 16, 16)]
FORWARD = False


def gather_bias(blk_ref, g_ref, own_sem, zs, zr, as_, ar_, bs, br, fs, fr, work=()):
    row, col, dev = my_place()
    core, z, y, x = col % 2, col // 2, row % 4, row // 4
    a_me = jnp.where(core == 0, y, x)
    b_me = jnp.where(core == 0, x, y)
    sibling = (row, z * 2 + 1 - core)
    work = list(work)

    def do_work():
        if work:
            work.pop(0)()

    def row_of(a, b):
        a, b = lax.rem(a, 4), lax.rem(b, 4)
        return jnp.where(core == 0, b * 4 + a, a * 4 + b)

    def part(half, start, size):
        return g_ref.at[half, pl.ds(start, size)]

    started = []

    def send(src, dst, ssem, rsem, device):
        copy = pltpu.make_async_remote_copy(
            src_ref=src, dst_ref=dst, send_sem=ssem, recv_sem=rsem, device_id=device, device_id_type=MESH
        )
        copy.start()
        started.append(copy)

    near = [(1, 0), (3, 0), (0, 1), (1, 1), (3, 1), (2, 0), (2, 1)]
    for step, flip in near:
        to_core = lax.rem(core + flip, 2)
        send(
            blk_ref.at[pl.ds(to_core, 1)],
            g_ref.at[pl.ds(to_core, 1), dev],
            zs.at[step * 2 + flip],
            zr.at[(4 - step) % 4 * 2 + flip],
            (row, lax.rem(z + step, 4) * 2 + to_core),
        )
    own = pltpu.make_async_copy(blk_ref.at[pl.ds(core, 1)], g_ref.at[pl.ds(core, 1), dev], own_sem.at[0])
    own.start()
    do_work()
    own.wait()
    for step, flip in near:
        source = row * 8 + lax.rem(z + step, 4) * 2 + lax.rem(core + flip, 2)
        drain(g_ref.at[pl.ds(core, 1), source], zr.at[step * 2 + flip])

    def block(da, db):
        return part(core, row_of(a_me + da, b_me + db) * 8, 8)

    def to_sibling(da, db):
        ref = block(da, db)
        send(ref, ref, fs.at[da * 4 + db], fr.at[da * 4 + db], sibling)

    def along_b(da, db, step):
        ref = block(da, db)
        rel = (db - step) % 4
        send(ref, ref, bs.at[da * 4 + rel], br.at[da * 4 + rel], (row_of(a_me, b_me + step), col))

    def spread(da):
        along_b(da, 0, 1)
        along_b(da, 0, 3)
        if not FORWARD:
            along_b(da, 0, 2)
        to_sibling(da, 0)

    for step in (1, 3, 2):
        ref = block(0, 0)
        send(ref, ref, as_.at[step], ar_.at[4 - step], (row_of(a_me + step, b_me), col))
    spread(0)
    do_work()
    for da in (1, 3, 2):
        drain(block(da, 0), ar_.at[da])
        spread(da)
    do_work()
    for da in (0, 1, 3, 2):
        for db in (3, 1):
            drain(block(da, db), br.at[da * 4 + db])
            if FORWARD and (db == 3) == (da in (0, 3)):
                along_b(da, db, 1 if db == 3 else 3)
            to_sibling(da, db)
    do_work()
    for da in (0, 1, 3, 2):
        drain(block(da, 2), br.at[da * 4 + 2])
        to_sibling(da, 2)
    while work:
        do_work()
    for db in (0, 3, 1, 2):
        for da in (0, 1, 3, 2):
            s_row = jnp.where(
                core == 1,
                lax.rem(x + db, 4) * 4 + lax.rem(y + da, 4),
                lax.rem(x + da, 4) * 4 + lax.rem(y + db, 4),
            )
            drain(part(1 - core, s_row * 8, 8), fr.at[da * 4 + db])
    for copy in started:
        copy.wait_send()


PROJECTED = (
    jax.ShapeDtypeStruct((4, 512, 128), BF16),
    jax.ShapeDtypeStruct((4, 128, 512), BF16),
    jax.ShapeDtypeStruct((4, 128, 512), BF16),
    jax.ShapeDtypeStruct((4, 128, 512), F32),
)


def project_line(line, normed, project_ref, k_ref, q_ref, v_ref, gate_ref):
    k_ref[line] = dot(normed, project_ref[:, 128:256]).astype(BF16)
    q_ref[line] = dot(project_ref[:, 0:128], normed, 0, 1).astype(BF16)
    both = dot(project_ref[:, 256:512], normed, 0, 1)
    v_ref[line] = both[:128].astype(BF16)
    gate_ref[line] = sigmoid(both[128:])


def start_kernel(x_ref, bias_w_ref, project_ref, g_ref, k_ref, q_ref, v_ref, gate_ref, blk32, blk, normed_buf, *sems):
    signals = signal_partners()
    inverse = 1.0 / bias_step(bias_w_ref)
    for line in range(4):
        normed = layer_norm(x_ref[line].astype(F32)).astype(BF16)
        normed_buf[line] = normed
        code_bias(blk32, line, bias_w_ref, inverse, normed)
    blk[...] = blk32[...].astype(jnp.int16)
    await_signals(signals)

    def work(line):
        project_line(line, normed_buf[line], project_ref, k_ref, q_ref, v_ref, gate_ref)

    gather_bias(blk, g_ref, *sems, work=[functools.partial(work, line) for line in range(4)])


BLK = [pltpu.VMEM((2, 2, 16, 128), jnp.int32), pltpu.VMEM((2, 2, 16, 128), jnp.int16)]


def start(x, bias_w, project):
    return pl.pallas_call(
        start_kernel,
        out_shape=(jax.ShapeDtypeStruct(G_SHAPE, jnp.int16),) + PROJECTED,
        in_specs=[vmem()] * 3,
        out_specs=(vmem(),) * 5,
        scratch_shapes=BLK + [pltpu.VMEM((4, 512, 128), BF16)] + GATHER_SEMS,
        compiler_params=pltpu.CompilerParams(
            collective_id=0, has_side_effects=True, vmem_limit_bytes=VMEM_LIMIT
        ),
        name="bias_gather",
    )(x, bias_w, project)


def all_to_all_some(src_ref, dst_ref, ssem, rsem, lsem, first, last):
    row, col, dev = my_place()

    def step(off, carry):
        dest = lax.rem(dev + off, DEVS)
        pltpu.make_async_remote_copy(
            src_ref=src_ref.at[dest],
            dst_ref=dst_ref.at[dev],
            send_sem=ssem,
            recv_sem=rsem,
            device_id=(dest // 8, dest % 8),
            device_id_type=MESH,
        ).start()
        return carry

    if first == 1:
        pltpu.make_async_copy(src_ref.at[dev], dst_ref.at[dev], lsem).start()
    lax.fori_loop(first, last, step, 0)


def all_to_all_start(*args):
    all_to_all_some(*args, 1, DEVS)


def all_to_all_recv(src_ref, dst_ref, ssem, rsem, lsem):
    drain(dst_ref.at[0], lsem)
    drain(dst_ref.at[pl.ds(0, DEVS - 1)], rsem)


def all_to_all_sent(src_ref, dst_ref, ssem, rsem, lsem):
    drain(src_ref.at[pl.ds(0, DEVS - 1)], ssem)


def middle_kernel(
    x_ref,
    mix_ref,
    output_ref,
    bias_w_ref,
    project_ref,
    g_ref,
    k_ref,
    q_ref,
    v_ref,
    gate_ref,
    cols_ref,
    line_buf,
    send_buf,
    tiles,
    cols_buf,
    blk32,
    blk,
    s0,
    s1,
    s2,
    *sems,
):
    signals = signal_all()
    inverse = 1.0 / bias_step(bias_w_ref)
    w_o = output_ref[...]
    for line in range(4):
        value = x_ref[line].astype(F32) + dot(mix_ref[line], w_o, 0, 0)
        value = value.astype(BF16).astype(F32)
        code_bias(blk32, line, bias_w_ref, inverse, layer_norm(value).astype(BF16))
        line_buf[line] = value
        for j in range(4):
            send_buf[pl.ds(line * 4 + j, 128, stride=16), :] = line_buf[line, pl.ds(j, 128, stride=4), :]
    blk[...] = blk32[...].astype(jnp.int16)
    tiles[...] = send_buf[...].reshape(128, 16, 128).astype(BF16)
    await_signals(signals)
    args = (tiles, cols_ref, s0, s1, s2)

    def project_all():
        all_to_all_recv(*args)
        cols_buf[...] = cols_ref[...].astype(F32).reshape(2048, 128)
        for line in range(4):
            normed = layer_norm(cols_buf[pl.ds(line, 512, stride=4), :]).astype(BF16)
            project_line(line, normed, project_ref, k_ref, q_ref, v_ref, gate_ref)

    work = [functools.partial(all_to_all_some, *args, lo, hi) for lo, hi in ((1, 33), (33, 81), (81, 128))]
    gather_bias(blk, g_ref, *sems, work=work + [project_all])
    all_to_all_sent(*args)


def middle(x, mix, output, bias_w, project):
    return pl.pallas_call(
        middle_kernel,
        out_shape=(jax.ShapeDtypeStruct(G_SHAPE, jnp.int16),)
        + PROJECTED
        + (jax.ShapeDtypeStruct((128, 16, 128), BF16),),
        in_specs=[vmem()] * 5,
        out_specs=(vmem(),) * 6,
        scratch_shapes=[
            pltpu.VMEM((4, 512, 128), F32),
            pltpu.VMEM((2048, 128), F32),
            pltpu.VMEM((128, 16, 128), BF16),
            pltpu.VMEM((2048, 128), F32),
        ]
        + BLK
        + [pltpu.SemaphoreType.DMA] * 3
        + GATHER_SEMS,
        compiler_params=pltpu.CompilerParams(
            collective_id=1, has_side_effects=True, vmem_limit_bytes=VMEM_LIMIT
        ),
        name="columns_and_bias",
    )(x, mix, output, bias_w, project)


def compact(flags):
    count = jnp.int32(0)
    picked = [jnp.int32(0)] * 4
    for tile in range(4):
        for place in range(4):
            hit = jnp.logical_and(flags[tile] > 0, count == place)
            picked[place] = jnp.where(hit, tile, picked[place])
        count = count + flags[tile]
    return picked, count


def attention_kernel(
    which, mask_ref, add_ref, g_ref, ids_ref, bias_w_ref, k_ref, q_ref, v_ref, gate_ref, mix_ref, bias_buf, code_buf, ids_buf
):
    row, _, _ = my_place()
    flags = [mask_ref[row // 4, t] if which == 0 else mask_ref[t, row // 4] for t in range(4)]
    scale = LOG2E * 32 ** (-0.5)
    ids = ids_ref[...].astype(F32)
    for tile in range(4):
        ids_buf[tile] = jnp.broadcast_to(ids[:, tile * 128 : (tile + 1) * 128], (128, 128)).T
    picked, count = compact(flags)
    steps = bias_step(bias_w_ref) * LOG2E
    adds = [add_ref[which, head] * LOG2E for head in range(4)]
    lanes = lax.broadcasted_iota(jnp.int32, (1, 128), 1) // 32
    head_masks = [jnp.where(lanes == head, 1.0, 0.0).astype(BF16) for head in range(4)]
    upper = lax.broadcasted_iota(jnp.int32, (64, 128), 0) < 32

    def run(tiles):
        def load_bias(place):
            tile = picked[place]
            if which == 0:
                code_buf[...] = g_ref[tile // 2, :, tile % 2].astype(F32).reshape(2048, 128)
            for q_tile in range(4):
                if which == 1:
                    got = g_ref[q_tile // 2, pl.ds(tile * 32, 32), q_tile % 2].astype(F32)
                    code_buf[0:512, :] = got.reshape(512, 128)
                same = ids_buf[tile] == ids[:, q_tile * 128 : (q_tile + 1) * 128]
                for head in range(4):
                    if which == 0:
                        code = code_buf[pl.ds(q_tile * 512 + head, 128, stride=4), :].T
                    else:
                        code = code_buf[pl.ds(head, 128, stride=4), :]
                    bias = code * steps[head : head + 1] + jnp.where(same, adds[head], 0.0)
                    bias_buf[head, place, :, q_tile * 128 : (q_tile + 1) * 128] = bias

        for place in range(tiles):
            load_bias(place)

        def body(step, carry):
            line, block = step // 2, step % 2
            q_at = pl.ds(pl.multiple_of(block * 256, 256), 256)
            q = q_ref[line, :, q_at]
            k_at = [pl.ds(pl.multiple_of(picked[place] * 128, 128), 128) for place in range(tiles)]
            scores = []
            for place in range(tiles):
                keys = k_ref[line, k_at[place], :]
                stacked = jnp.concatenate([keys * head_masks[head] for head in range(4)], axis=0)
                scores.append(dot(stacked, q))
            for pair in range(2):
                weights, totals = [], []
                for head in (2 * pair, 2 * pair + 1):
                    logits = [
                        scores[place][head * 128 : (head + 1) * 128] * scale + bias_buf[head, place, :, q_at]
                        for place in range(tiles)
                    ]
                    peak = functools.reduce(jnp.maximum, [jnp.max(s, axis=0, keepdims=True) for s in logits])
                    own = [jnp.exp2(s - peak) for s in logits]
                    totals.append(functools.reduce(jnp.add, [jnp.sum(w, axis=0, keepdims=True) for w in own]))
                    weights.append([w.astype(BF16) for w in own])
                rows = pl.ds(64 * pair, 64)
                mixed = None
                for place in range(tiles):
                    v = v_ref[line, rows, k_at[place]]
                    zero = jnp.zeros_like(v)
                    spread = jnp.concatenate([jnp.where(upper, v, zero), jnp.where(upper, zero, v)], axis=1)
                    term = dot(spread, jnp.concatenate([weights[0][place], weights[1][place]], axis=0))
                    mixed = term if mixed is None else mixed + term
                inverse = [1.0 / total for total in totals]
                for sub in range(2):
                    at = pl.ds(64 * pair + 32 * sub, 32)
                    gated = mixed[32 * sub : 32 * sub + 32] * inverse[sub] * gate_ref[line, at, q_at]
                    mix_ref[line, at, q_at] = gated.astype(BF16)
            return carry

        lax.fori_loop(0, 8, body, 0)

    for tiles in range(1, 5):
        pl.when(count == tiles)(functools.partial(run, tiles))


def attention(which, mask, add, g, ids, bias_w, projected):
    return pl.pallas_call(
        functools.partial(attention_kernel, which),
        out_shape=jax.ShapeDtypeStruct((4, 128, 512), BF16),
        in_specs=[smem(), smem()] + [vmem()] * 7,
        out_specs=vmem(),
        scratch_shapes=[
            pltpu.VMEM((4, 4, 128, 512), F32),
            pltpu.VMEM((2048, 128), F32),
            pltpu.VMEM((4, 128, 128), F32),
        ],
        compiler_params=pltpu.CompilerParams(vmem_limit_bytes=VMEM_LIMIT),
        name=("row_attention", "col_attention")[which],
    )(mask, add, g, ids, bias_w, *projected)


def triangle_kernel(
    mask_ref,
    cols_ref,
    mix_ref,
    output_ref,
    left_ref,
    right_ref,
    gate_w_ref,
    out_w_ref,
    out_ref,
    cols_buf,
    edge_ref,
    second_ref,
    edge_in,
    second_in,
    edge_buf,
    prod_send,
    prod_in,
    x_buf,
    gate_buf,
    norm_buf,
    es,
    er,
    el,
    ss,
    sr,
    sl,
    ps,
    pr,
    pl_,
):
    row, col, dev = my_place()
    signals = signal_all()
    flags = [mask_ref[tile, row // 4].astype(F32) for tile in range(4)]
    cols_buf[...] = cols_ref[...].astype(F32).reshape(2048, 128)
    w_o = output_ref[...]
    for line in range(4):
        value = cols_buf[pl.ds(line, 512, stride=4), :] + dot(mix_ref[line], w_o, 0, 0)
        rounded = value.astype(BF16)
        second_ref[:, line * 32 : (line + 1) * 32, :] = rounded.reshape(16, 32, 128)
        normed = layer_norm(rounded.astype(F32)).astype(BF16)
        for side, w_ref in enumerate((left_ref, right_ref)):
            both = dot(w_ref[...], normed, 0, 1)
            act = sigmoid(both[128:]) * both[:128]
            for tile in range(4):
                edge_buf[pl.ds(line * 8 + side * 4 + tile, 128, stride=32), :] = (
                    act[:, tile * 128 : (tile + 1) * 128] * flags[tile]
                )
    edge_ref[...] = edge_buf[...].reshape(128, 32, 128).astype(BF16)
    await_signals(signals)
    edges = (edge_ref, edge_in, es, er, el)
    all_to_all_start(*edges)
    slot = lax.rem(dev, 16)
    grid_col = dev // 16

    def send_second(step, carry):
        to_row = lax.rem(row + step, 16)

        @pl.when(jnp.logical_and(to_row == row, grid_col == col))
        def _():
            pltpu.make_async_copy(second_ref.at[to_row], second_in.at[slot], sl).start()

        @pl.when(jnp.logical_not(jnp.logical_and(to_row == row, grid_col == col)))
        def _():
            pltpu.make_async_remote_copy(
                src_ref=second_ref.at[to_row],
                dst_ref=second_in.at[slot],
                send_sem=ss,
                recv_sem=sr,
                device_id=(to_row, grid_col),
                device_id_type=MESH,
            ).start()

        return carry

    all_to_all_recv(*edges)
    lax.fori_loop(0, 16, send_second, 0)
    edge_buf[...] = edge_in[...].astype(F32).reshape(4096, 128)
    right = jnp.concatenate([edge_buf[pl.ds(4 + tile, 512, stride=8), :] for tile in range(4)], axis=1).astype(BF16)
    low = lax.broadcasted_iota(jnp.int32, (16, 128), 1) < 64
    for tile in range(4):
        left = edge_buf[pl.ds(tile, 512, stride=8), :].astype(BF16)
        product = dot(left, right, 0, 0)
        for sub in range(4):
            for t in range(4):
                a = product[sub * 32 : sub * 32 + 16, t * 128 : (t + 1) * 128]
                b = product[sub * 32 + 16 : sub * 32 + 32, t * 128 : (t + 1) * 128]
                block = (tile * 4 + sub) * 8 + 2 * t
                prod_send[block] = jnp.where(low, a, pltpu.roll(b, 64, 1)).astype(BF16)
                prod_send[block + 1] = jnp.where(low, pltpu.roll(a, 64, 1), b).astype(BF16)
    products = (prod_send, prod_in, ps, pr, pl_)
    all_to_all_start(*products)

    own_sent = grid_col == col

    @pl.when(own_sent)
    def _():
        drain(second_in.at[0], sl)
        drain(second_in.at[pl.ds(0, 15)], sr)
        drain(second_ref.at[pl.ds(0, 15)], ss)

    @pl.when(jnp.logical_not(own_sent))
    def _():
        drain(second_in, sr)
        drain(second_ref, ss)

    gate_w = gate_w_ref[...]

    def gates(j, carry):
        at = pl.multiple_of(j * 128, 128)
        x = second_in[j].astype(F32)
        gate = sigmoid(dot(layer_norm(x).astype(BF16), gate_w))
        for sub in range(4):
            x_buf[pl.ds(j * 4 + sub, 32, stride=64), :] = x[sub * 32 : (sub + 1) * 32]
            gate_buf[pl.ds(j * 4 + sub, 32, stride=64), :] = gate[sub * 32 : (sub + 1) * 32]
        return carry

    lax.fori_loop(0, 16, gates, 0)
    all_to_all_recv(*products)
    product = prod_in[...].astype(F32)
    center = product - jnp.mean(product, axis=0, keepdims=True)
    spread = jnp.mean(center * center, axis=0, keepdims=True)
    norm_buf[...] = (center * lax.rsqrt(spread + 1e-05)).reshape(2048, 128)
    out_w = out_w_ref[...]
    for s in range(16):
        update = dot(norm_buf[pl.ds(s, 128, stride=16), :].astype(BF16), out_w, 0, 0)
        for half in range(2):
            i = half * 16 + s
            at = pl.ds(i * 64, 64)
            out_ref[i] = (x_buf[at, :] + gate_buf[at, :] * update[half * 64 : (half + 1) * 64]).astype(BF16)
    all_to_all_sent(*edges)
    all_to_all_sent(*products)


def triangle(mask, cols, mix, output, left, right, gate_w, out_w):
    return pl.pallas_call(
        triangle_kernel,
        out_shape=jax.ShapeDtypeStruct((32, 64, 128), BF16),
        in_specs=[smem()] + [vmem()] * 7,
        out_specs=vmem(),
        scratch_shapes=[
            pltpu.VMEM((2048, 128), F32),
            pltpu.VMEM((128, 32, 128), BF16),
            pltpu.VMEM((16, 128, 128), BF16),
            pltpu.VMEM((128, 32, 128), BF16),
            pltpu.VMEM((16, 128, 128), BF16),
            pltpu.VMEM((4096, 128), F32),
            pltpu.VMEM((128, 16, 128), BF16),
            pltpu.VMEM((128, 16, 128), BF16),
            pltpu.VMEM((2048, 128), F32),
            pltpu.VMEM((2048, 128), F32),
            pltpu.VMEM((2048, 128), F32),
        ]
        + [pltpu.SemaphoreType.DMA] * 9,
        compiler_params=pltpu.CompilerParams(
            collective_id=2, has_side_effects=True, vmem_limit_bytes=VMEM_LIMIT
        ),
        name="triangle",
    )(mask, cols, mix, output, left, right, gate_w, out_w)


def shards(
    pair_rep,
    tile_mask,
    chain_ids,
    chain_bias,
    row_project,
    row_bias_proj,
    row_output,
    col_project,
    col_bias_proj,
    col_output,
    tri_left,
    tri_right,
    tri_gate,
    tri_output,
):
    ids = chain_ids.reshape(1, 512)
    row_w, col_w = row_bias_proj.T, col_bias_proj.T
    g_rows, *projected = start(pair_rep, row_w, row_project)
    mix = attention(0, tile_mask, chain_bias, g_rows, ids, row_w, projected)
    g_cols, *projected, cols = middle(pair_rep, mix, row_output, col_w, col_project)
    mix = attention(1, tile_mask, chain_bias, g_cols, ids, col_w, projected)
    return triangle(tile_mask, cols, mix, col_output, tri_left, tri_right, tri_gate, tri_output)


def solution(mesh):
    spec = P(("row", "col"), None, None)
    return jax.shard_map(
        shards,
        mesh=mesh,
        in_specs=(spec,) + (P(),) * 13,
        out_specs=P("row", "col", None),
        check_vma=False,
    )
```

```python
import functools
import math

import jax
import jax.numpy as jnp
from jax import lax
from jax.experimental import pallas as pl
from jax.experimental.pallas import tpu as pltpu
from jax.sharding import PartitionSpec as P

MESH = pl.DeviceIdType.MESH
F32 = jnp.float32
BF16 = jnp.bfloat16
DEVS = 128
LOG2E = 1.4426950408889634
VMEM_LIMIT = 24 * 2**20


def vmem():
    return pl.BlockSpec(memory_space=pltpu.VMEM)


def hbm():
    return pl.BlockSpec(memory_space=pltpu.HBM)


def smem():
    return pl.BlockSpec(memory_space=pltpu.SMEM)


def layer_norm(values):
    center = values - jnp.mean(values, axis=-1, keepdims=True)
    spread = jnp.mean(center * center, axis=-1, keepdims=True)
    return center * lax.rsqrt(spread + 1e-05)


def dot(a, b, ca=1, cb=0):
    return lax.dot_general(a, b, (((ca,), (cb,)), ((), ())), preferred_element_type=F32)


def sigmoid(x):
    return 1.0 / (1.0 + jnp.exp(-x))


def my_place():
    row, col = lax.axis_index("row"), lax.axis_index("col")
    return row, col, row * 8 + col


def at_offset(offset):
    row, col, _ = my_place()
    x = lax.rem(row // 4 + offset // 32, 4)
    y = lax.rem(row % 4 + offset // 8 % 4, 4)
    z = lax.rem(col // 2 + offset // 2 % 4, 4)
    return ((x * 4 + y) * 4 + z) * 2 + lax.rem(col % 2 + offset % 2, 2)


def drain(ref, sem):
    pltpu.make_async_copy(ref, ref, sem).wait()


def bias_step(w_ref):
    w = w_ref[...].astype(F32)
    length = jnp.sqrt(jnp.sum(w * w, axis=1, keepdims=True))
    return jnp.maximum(length, 1e-20) * (11.4 / 32766.0)


def code_bias(blk32, line, w_ref, inverse, normed):
    coded = jnp.round(dot(w_ref[...], normed, 1, 1) * inverse).astype(jnp.int32)
    for tile in range(4):
        blk32[tile // 2, tile % 2, line * 4 : line * 4 + 4, :] = coded[:, tile * 128 : (tile + 1) * 128]


def signal_partners():
    row, col, _ = my_place()
    core, z, y, x = col % 2, col // 2, row % 4, row // 4
    partners = []
    for step in range(4):
        for flip in range(2):
            if step or flip:
                partners.append((row, lax.rem(z + step, 4) * 2 + lax.rem(core + flip, 2)))
    for step in (1, 2, 3):
        partners.append((x * 4 + lax.rem(y + step, 4), col))
        partners.append((lax.rem(x + step, 4) * 4 + y, col))
    barrier = pltpu.get_barrier_semaphore()
    for partner in partners:
        pl.semaphore_signal(barrier, inc=1, device_id=partner, device_id_type=MESH)
    return len(partners)


class Everyone:
    def __init__(self, second, third):
        self.second, self.third = second, third
        self.count = signal_partners()

    def next_round(self):
        row, col, _ = my_place()
        x, y = row // 4, row % 4
        await_signals(self.count)
        for step in (1, 2, 3):
            for to in (x * 4 + lax.rem(y + step, 4), lax.rem(x + step, 4) * 4 + y):
                pl.semaphore_signal(self.second, inc=1, device_id=(to, col), device_id_type=MESH)

    def last_round(self):
        row, col, _ = my_place()
        pl.semaphore_wait(self.second, 6)
        for step in range(1, 8):
            pl.semaphore_signal(self.third, inc=1, device_id=(row, lax.rem(col + step, 8)), device_id_type=MESH)

    def wait(self):
        pl.semaphore_wait(self.third, 7)


EVERYONE = [pltpu.SemaphoreType.REGULAR] * 2


def await_signals(count):
    pl.semaphore_wait(pltpu.get_barrier_semaphore(), count)


G_SHAPE = (2, 128, 2, 16, 128)
GATHER_SEMS = [pltpu.SemaphoreType.DMA((n,)) for n in (1, 8, 8, 4, 4, 16, 16, 16, 16)]
FORWARD = False


def gather_bias(blk_ref, g_ref, own_sem, zs, zr, as_, ar_, bs, br, fs, fr, work=()):
    row, col, dev = my_place()
    core, z, y, x = col % 2, col // 2, row % 4, row // 4
    a_me = jnp.where(core == 0, y, x)
    b_me = jnp.where(core == 0, x, y)
    sibling = (row, z * 2 + 1 - core)
    work = list(work)

    def do_work():
        if work:
            work.pop(0)()

    def row_of(a, b):
        a, b = lax.rem(a, 4), lax.rem(b, 4)
        return jnp.where(core == 0, b * 4 + a, a * 4 + b)

    def part(half, start, size):
        return g_ref.at[half, pl.ds(start, size)]

    started = []

    def send(src, dst, ssem, rsem, device):
        copy = pltpu.make_async_remote_copy(
            src_ref=src, dst_ref=dst, send_sem=ssem, recv_sem=rsem, device_id=device, device_id_type=MESH
        )
        copy.start()
        started.append(copy)

    near = [(1, 0), (3, 0), (0, 1), (1, 1), (3, 1), (2, 0), (2, 1)]
    for step, flip in near:
        to_core = lax.rem(core + flip, 2)
        send(
            blk_ref.at[pl.ds(to_core, 1)],
            g_ref.at[pl.ds(to_core, 1), dev],
            zs.at[step * 2 + flip],
            zr.at[(4 - step) % 4 * 2 + flip],
            (row, lax.rem(z + step, 4) * 2 + to_core),
        )
    own = pltpu.make_async_copy(blk_ref.at[pl.ds(core, 1)], g_ref.at[pl.ds(core, 1), dev], own_sem.at[0])
    own.start()
    do_work()
    own.wait()
    for step, flip in near:
        source = row * 8 + lax.rem(z + step, 4) * 2 + lax.rem(core + flip, 2)
        drain(g_ref.at[pl.ds(core, 1), source], zr.at[step * 2 + flip])

    def block(da, db):
        return part(core, row_of(a_me + da, b_me + db) * 8, 8)

    def to_sibling(da, db):
        ref = block(da, db)
        send(ref, ref, fs.at[da * 4 + db], fr.at[da * 4 + db], sibling)

    def along_b(da, db, step):
        ref = block(da, db)
        rel = (db - step) % 4
        send(ref, ref, bs.at[da * 4 + rel], br.at[da * 4 + rel], (row_of(a_me, b_me + step), col))

    def spread(da):
        along_b(da, 0, 1)
        along_b(da, 0, 3)
        if not FORWARD:
            along_b(da, 0, 2)
        to_sibling(da, 0)

    for step in (1, 3, 2):
        ref = block(0, 0)
        send(ref, ref, as_.at[step], ar_.at[4 - step], (row_of(a_me + step, b_me), col))
    spread(0)
    do_work()
    for da in (1, 3, 2):
        drain(block(da, 0), ar_.at[da])
        spread(da)
    do_work()
    for da in (0, 1, 3, 2):
        for db in (3, 1):
            drain(block(da, db), br.at[da * 4 + db])
            if FORWARD and (db == 3) == (da in (0, 3)):
                along_b(da, db, 1 if db == 3 else 3)
            to_sibling(da, db)
    do_work()
    for da in (0, 1, 3, 2):
        drain(block(da, 2), br.at[da * 4 + 2])
        to_sibling(da, 2)
    while work:
        do_work()
    for db in (0, 3, 1, 2):
        for da in (0, 1, 3, 2):
            s_row = jnp.where(
                core == 1,
                lax.rem(x + db, 4) * 4 + lax.rem(y + da, 4),
                lax.rem(x + da, 4) * 4 + lax.rem(y + db, 4),
            )
            drain(part(1 - core, s_row * 8, 8), fr.at[da * 4 + db])
    for copy in started:
        copy.wait_send()


PROJECTED = (
    jax.ShapeDtypeStruct((4, 512, 128), BF16),
    jax.ShapeDtypeStruct((4, 128, 512), BF16),
    jax.ShapeDtypeStruct((4, 128, 512), BF16),
    jax.ShapeDtypeStruct((4, 128, 512), F32),
)


def project_line(line, normed, project_ref, k_ref, q_ref, v_ref, gate_ref):
    k_ref[line] = dot(normed, project_ref[:, 128:256]).astype(BF16)
    q_ref[line] = dot(project_ref[:, 0:128], normed, 0, 1).astype(BF16)
    both = dot(project_ref[:, 256:512], normed, 0, 1)
    v_ref[line] = both[:128].astype(BF16)
    gate_ref[line] = sigmoid(both[128:])


BLK = [pltpu.VMEM((2, 2, 16, 128), jnp.int32), pltpu.VMEM((2, 2, 16, 128), jnp.int16)]
STEPS = jax.ShapeDtypeStruct((4, 128), F32)


def start_kernel(
    x_hbm,
    bias_w_hbm,
    project_hbm,
    mask_hbm,
    add_hbm,
    ids_hbm,
    g_ref,
    k_ref,
    q_ref,
    v_ref,
    gate_ref,
    steps_ref,
    mask_ref,
    add_ref,
    ids_ref,
    x_buf,
    bias_w_buf,
    project_buf,
    blk32,
    blk,
    normed_buf,
    loaded,
    *sems,
):
    loads = [pltpu.make_async_copy(bias_w_hbm, bias_w_buf, loaded.at[0])]
    loads += [pltpu.make_async_copy(x_hbm.at[line], x_buf.at[line], loaded.at[1 + line]) for line in range(4)]
    loads.append(pltpu.make_async_copy(project_hbm, project_buf, loaded.at[5]))
    pairs = ((mask_hbm, mask_ref), (add_hbm, add_ref), (ids_hbm, ids_ref))
    loads += [pltpu.make_async_copy(src, dst, loaded.at[6 + i]) for i, (src, dst) in enumerate(pairs)]
    for load in loads:
        load.start()
    signals = signal_partners()
    loads[0].wait()
    step = bias_step(bias_w_buf)
    steps_ref[...] = jnp.broadcast_to(step, (4, 128))
    inverse = 1.0 / step
    for line in range(4):
        loads[1 + line].wait()
        normed = layer_norm(x_buf[line].astype(F32)).astype(BF16)
        normed_buf[line] = normed
        code_bias(blk32, line, bias_w_buf, inverse, normed)
    blk[...] = blk32[...].astype(jnp.int16)
    await_signals(signals)

    def work(line):
        if line == 0:
            for load in loads[5:]:
                load.wait()
        project_line(line, normed_buf[line], project_buf, k_ref, q_ref, v_ref, gate_ref)

    gather_bias(blk, g_ref, *sems, work=[functools.partial(work, line) for line in range(4)])


def start(x, bias_w, project, mask, add, ids):
    return pl.pallas_call(
        start_kernel,
        out_shape=(jax.ShapeDtypeStruct(G_SHAPE, jnp.int16),)
        + PROJECTED
        + (STEPS,)
        + tuple(jax.ShapeDtypeStruct(a.shape, a.dtype) for a in (mask, add, ids)),
        in_specs=[hbm()] * 6,
        out_specs=(vmem(),) * 9,
        scratch_shapes=[
            pltpu.VMEM((4, 512, 128), BF16),
            pltpu.VMEM((4, 128), BF16),
            pltpu.VMEM((128, 512), BF16),
        ]
        + BLK
        + [pltpu.VMEM((4, 512, 128), BF16), pltpu.SemaphoreType.DMA((9,))]
        + GATHER_SEMS,
        compiler_params=pltpu.CompilerParams(
            collective_id=0, has_side_effects=True, vmem_limit_bytes=VMEM_LIMIT
        ),
        name="bias_gather",
    )(x, bias_w, project, mask, add, ids)


def all_to_all_some(src_ref, dst_ref, ssem, rsem, lsem, first, last):
    row, col, dev = my_place()

    def step(i, carry):
        dest = at_offset(lax.rem(i * 37, DEVS))
        pltpu.make_async_remote_copy(
            src_ref=src_ref.at[dest],
            dst_ref=dst_ref.at[dev],
            send_sem=ssem,
            recv_sem=rsem,
            device_id=(dest // 8, dest % 8),
            device_id_type=MESH,
        ).start()
        return carry

    if first == 1:
        pltpu.make_async_copy(src_ref.at[dev], dst_ref.at[dev], lsem).start()
    lax.fori_loop(first, last, step, 0)


def all_to_all_start(*args):
    all_to_all_some(*args, 1, DEVS)


def all_to_all_recv(src_ref, dst_ref, ssem, rsem, lsem):
    drain(dst_ref.at[0], lsem)
    drain(dst_ref.at[pl.ds(0, DEVS - 1)], rsem)


def all_to_all_sent(src_ref, dst_ref, ssem, rsem, lsem):
    drain(src_ref.at[pl.ds(0, DEVS - 1)], ssem)


def middle_kernel(
    x_ref,
    mix_ref,
    output_ref,
    bias_w_ref,
    project_ref,
    g_ref,
    k_ref,
    q_ref,
    v_ref,
    gate_ref,
    steps_ref,
    cols_ref,
    line_buf,
    send_buf,
    tiles,
    cols_buf,
    blk32,
    blk,
    second_round,
    third_round,
    s0,
    s1,
    s2,
    *sems,
):
    everyone = Everyone(second_round, third_round)
    step = bias_step(bias_w_ref)
    steps_ref[...] = jnp.broadcast_to(step, (4, 128))
    inverse = 1.0 / step
    w_o = output_ref[...]
    for line in range(4):
        value = x_ref[line].astype(F32) + dot(mix_ref[line], w_o, 0, 0)
        value = value.astype(BF16).astype(F32)
        code_bias(blk32, line, bias_w_ref, inverse, layer_norm(value).astype(BF16))
        line_buf[line] = value
        for j in range(4):
            send_buf[pl.ds(line * 4 + j, 128, stride=16), :] = line_buf[line, pl.ds(j, 128, stride=4), :]
        if line == 1:
            everyone.next_round()
        if line == 3:
            everyone.last_round()
    blk[...] = blk32[...].astype(jnp.int16)
    tiles[...] = send_buf[...].reshape(128, 16, 128).astype(BF16)
    everyone.wait()
    args = (tiles, cols_ref, s0, s1, s2)

    def project_all():
        all_to_all_recv(*args)
        cols_buf[...] = cols_ref[...].astype(F32).reshape(2048, 128)
        for line in range(4):
            normed = layer_norm(cols_buf[pl.ds(line, 512, stride=4), :]).astype(BF16)
            project_line(line, normed, project_ref, k_ref, q_ref, v_ref, gate_ref)

    work = [functools.partial(all_to_all_some, *args, lo, hi) for lo, hi in ((1, 33), (33, 81), (81, 128))]
    gather_bias(blk, g_ref, *sems, work=work + [project_all])
    all_to_all_sent(*args)


def middle(x, mix, output, bias_w, project):
    return pl.pallas_call(
        middle_kernel,
        out_shape=(jax.ShapeDtypeStruct(G_SHAPE, jnp.int16),)
        + PROJECTED
        + (STEPS, jax.ShapeDtypeStruct((128, 16, 128), BF16)),
        in_specs=[vmem()] * 5,
        out_specs=(vmem(),) * 7,
        scratch_shapes=[
            pltpu.VMEM((4, 512, 128), F32),
            pltpu.VMEM((2048, 128), F32),
            pltpu.VMEM((128, 16, 128), BF16),
            pltpu.VMEM((2048, 128), F32),
        ]
        + BLK
        + EVERYONE
        + [pltpu.SemaphoreType.DMA] * 3
        + GATHER_SEMS,
        compiler_params=pltpu.CompilerParams(
            collective_id=1, has_side_effects=True, vmem_limit_bytes=VMEM_LIMIT
        ),
        name="columns_and_bias",
    )(x, mix, output, bias_w, project)


def compact(flags):
    count = jnp.int32(0)
    picked = [jnp.int32(0)] * 4
    for tile in range(4):
        for place in range(4):
            hit = jnp.logical_and(flags[tile] > 0, count == place)
            picked[place] = jnp.where(hit, tile, picked[place])
        count = count + flags[tile]
    return picked, count


def attention_kernel(
    which, mask_ref, add_ref, g_ref, ids_ref, steps_ref, k_ref, q_ref, v_ref, gate_ref, mix_ref, bias_buf, code_buf, ids_buf
):
    row, _, _ = my_place()
    flags = [mask_ref[row // 4, t] if which == 0 else mask_ref[t, row // 4] for t in range(4)]
    scale = LOG2E * 32 ** (-0.5)
    ids = ids_ref[...].astype(F32)
    for tile in range(4):
        ids_buf[tile] = jnp.broadcast_to(ids[:, tile * 128 : (tile + 1) * 128], (128, 128)).T
    picked, count = compact(flags)
    steps = steps_ref[...] * LOG2E
    adds = [add_ref[which, head] * LOG2E for head in range(4)]
    lanes = lax.broadcasted_iota(jnp.int32, (1, 128), 1) // 32
    head_masks = [jnp.where(lanes == head, 1.0, 0.0).astype(BF16) for head in range(4)]
    upper = lax.broadcasted_iota(jnp.int32, (64, 128), 0) < 32

    def run(tiles):
        def load_bias(place):
            tile = picked[place]
            if which == 0:
                code_buf[...] = g_ref[tile // 2, :, tile % 2].astype(F32).reshape(2048, 128)
            for q_tile in range(4):
                if which == 1:
                    got = g_ref[q_tile // 2, pl.ds(tile * 32, 32), q_tile % 2].astype(F32)
                    code_buf[0:512, :] = got.reshape(512, 128)
                same = ids_buf[tile] == ids[:, q_tile * 128 : (q_tile + 1) * 128]
                for head in range(4):
                    if which == 0:
                        code = code_buf[pl.ds(q_tile * 512 + head, 128, stride=4), :].T
                    else:
                        code = code_buf[pl.ds(head, 128, stride=4), :]
                    bias = code * steps[head : head + 1] + jnp.where(same, adds[head], 0.0)
                    bias_buf[head, place, :, q_tile * 128 : (q_tile + 1) * 128] = bias

        for place in range(tiles):
            load_bias(place)

        def body(step, carry):
            line, block = step // 2, step % 2
            q_at = pl.ds(pl.multiple_of(block * 256, 256), 256)
            q = q_ref[line, :, q_at]
            k_at = [pl.ds(pl.multiple_of(picked[place] * 128, 128), 128) for place in range(tiles)]
            scores = []
            for place in range(tiles):
                keys = k_ref[line, k_at[place], :]
                stacked = jnp.concatenate([keys * head_masks[head] for head in range(4)], axis=0)
                scores.append(dot(stacked, q))
            for pair in range(2):
                weights, totals = [], []
                for head in (2 * pair, 2 * pair + 1):
                    logits = [
                        scores[place][head * 128 : (head + 1) * 128] * scale + bias_buf[head, place, :, q_at]
                        for place in range(tiles)
                    ]
                    peak = functools.reduce(jnp.maximum, [jnp.max(s, axis=0, keepdims=True) for s in logits])
                    own = [jnp.exp2(s - peak) for s in logits]
                    totals.append(functools.reduce(jnp.add, [jnp.sum(w, axis=0, keepdims=True) for w in own]))
                    weights.append([w.astype(BF16) for w in own])
                rows = pl.ds(64 * pair, 64)
                mixed = None
                for place in range(tiles):
                    v = v_ref[line, rows, k_at[place]]
                    zero = jnp.zeros_like(v)
                    spread = jnp.concatenate([jnp.where(upper, v, zero), jnp.where(upper, zero, v)], axis=1)
                    term = dot(spread, jnp.concatenate([weights[0][place], weights[1][place]], axis=0))
                    mixed = term if mixed is None else mixed + term
                inverse = [1.0 / total for total in totals]
                for sub in range(2):
                    at = pl.ds(64 * pair + 32 * sub, 32)
                    gated = mixed[32 * sub : 32 * sub + 32] * inverse[sub] * gate_ref[line, at, q_at]
                    mix_ref[line, at, q_at] = gated.astype(BF16)
            return carry

        lax.fori_loop(0, 8, body, 0)

    for tiles in range(1, 5):
        pl.when(count == tiles)(functools.partial(run, tiles))


def attention(which, mask, add, g, ids, steps, projected):
    return pl.pallas_call(
        functools.partial(attention_kernel, which),
        out_shape=jax.ShapeDtypeStruct((4, 128, 512), BF16),
        in_specs=[smem(), smem()] + [vmem()] * 7,
        out_specs=vmem(),
        scratch_shapes=[
            pltpu.VMEM((4, 4, 128, 512), F32),
            pltpu.VMEM((2048, 128), F32),
            pltpu.VMEM((4, 128, 128), F32),
        ],
        compiler_params=pltpu.CompilerParams(vmem_limit_bytes=VMEM_LIMIT),
        name=("row_attention", "col_attention")[which],
    )(mask, add, g, ids, steps, *projected)


def triangle_kernel(
    mask_ref,
    cols_ref,
    mix_ref,
    output_ref,
    left_ref,
    right_ref,
    gate_w_ref,
    out_w_ref,
    out_ref,
    cols_buf,
    edge_ref,
    second_ref,
    edge_in,
    second_in,
    edge_buf,
    prod_send,
    prod_in,
    x_buf,
    gate_buf,
    norm_buf,
    es,
    er,
    el,
    ss,
    sr,
    sl,
    ps,
    pr,
    pl_,
    second_round,
    third_round,
):
    row, col, dev = my_place()
    everyone = Everyone(second_round, third_round)
    flags = [mask_ref[tile, row // 4].astype(F32) for tile in range(4)]
    cols_buf[...] = cols_ref[...].astype(F32).reshape(2048, 128)
    w_o = output_ref[...]
    for line in range(4):
        value = cols_buf[pl.ds(line, 512, stride=4), :] + dot(mix_ref[line], w_o, 0, 0)
        rounded = value.astype(BF16)
        second_ref[:, line * 32 : (line + 1) * 32, :] = rounded.reshape(16, 32, 128)
        normed = layer_norm(rounded.astype(F32)).astype(BF16)
        for side, w_ref in enumerate((left_ref, right_ref)):
            both = dot(w_ref[...], normed, 0, 1)
            act = sigmoid(both[128:]) * both[:128]
            for tile in range(4):
                edge_buf[pl.ds(line * 8 + side * 4 + tile, 128, stride=32), :] = (
                    act[:, tile * 128 : (tile + 1) * 128] * flags[tile]
                )
        if line == 1:
            everyone.next_round()
        if line == 3:
            everyone.last_round()
    edge_ref[...] = edge_buf[...].reshape(128, 32, 128).astype(BF16)
    everyone.wait()
    edges = (edge_ref, edge_in, es, er, el)
    all_to_all_start(*edges)
    slot = lax.rem(dev, 16)
    grid_col = dev // 16

    def send_second(step, carry):
        to_row = lax.rem(row + step, 16)

        @pl.when(jnp.logical_and(to_row == row, grid_col == col))
        def _():
            pltpu.make_async_copy(second_ref.at[to_row], second_in.at[slot], sl).start()

        @pl.when(jnp.logical_not(jnp.logical_and(to_row == row, grid_col == col)))
        def _():
            pltpu.make_async_remote_copy(
                src_ref=second_ref.at[to_row],
                dst_ref=second_in.at[slot],
                send_sem=ss,
                recv_sem=sr,
                device_id=(to_row, grid_col),
                device_id_type=MESH,
            ).start()

        return carry

    all_to_all_recv(*edges)
    lax.fori_loop(0, 16, send_second, 0)
    edge_buf[...] = edge_in[...].astype(F32).reshape(4096, 128)
    right = jnp.concatenate([edge_buf[pl.ds(4 + tile, 512, stride=8), :] for tile in range(4)], axis=1).astype(BF16)
    low = lax.broadcasted_iota(jnp.int32, (16, 128), 1) < 64
    products = (prod_send, prod_in, ps, pr, pl_)

    def send_product(slab, first):
        def step(i, carry):
            dest = at_offset(slab * 32 + lax.rem(i * 13, 32))
            pltpu.make_async_remote_copy(
                src_ref=prod_send.at[dest],
                dst_ref=prod_in.at[dev],
                send_sem=ps,
                recv_sem=pr,
                device_id=(dest // 8, dest % 8),
                device_id_type=MESH,
            ).start()
            return carry

        lax.fori_loop(first, 32, step, 0)

    for slab in range(4):
        tile = lax.rem(row // 4 + slab, 4)
        left = edge_buf[pl.ds(tile, 512, stride=8), :].astype(BF16)
        product = dot(left, right, 0, 0)
        for sub in range(4):
            for t in range(4):
                a = product[sub * 32 : sub * 32 + 16, t * 128 : (t + 1) * 128]
                b = product[sub * 32 + 16 : sub * 32 + 32, t * 128 : (t + 1) * 128]
                block = tile * 32 + sub * 8 + 2 * t
                prod_send[block] = jnp.where(low, a, pltpu.roll(b, 64, 1)).astype(BF16)
                prod_send[block + 1] = jnp.where(low, pltpu.roll(a, 64, 1), b).astype(BF16)
        if slab == 0:
            pltpu.make_async_copy(prod_send.at[dev], prod_in.at[dev], pl_).start()
        send_product(slab, 1 if slab == 0 else 0)

    own_sent = grid_col == col

    @pl.when(own_sent)
    def _():
        drain(second_in.at[0], sl)
        drain(second_in.at[pl.ds(0, 15)], sr)
        drain(second_ref.at[pl.ds(0, 15)], ss)

    @pl.when(jnp.logical_not(own_sent))
    def _():
        drain(second_in, sr)
        drain(second_ref, ss)

    gate_w = gate_w_ref[...]

    def gates(j, carry):
        at = pl.multiple_of(j * 128, 128)
        x = second_in[j].astype(F32)
        gate = sigmoid(dot(layer_norm(x).astype(BF16), gate_w))
        for sub in range(4):
            x_buf[pl.ds(j * 4 + sub, 32, stride=64), :] = x[sub * 32 : (sub + 1) * 32]
            gate_buf[pl.ds(j * 4 + sub, 32, stride=64), :] = gate[sub * 32 : (sub + 1) * 32]
        return carry

    lax.fori_loop(0, 16, gates, 0)
    all_to_all_recv(*products)
    product = prod_in[...].astype(F32)
    center = product - jnp.mean(product, axis=0, keepdims=True)
    spread = jnp.mean(center * center, axis=0, keepdims=True)
    norm_buf[...] = (center * lax.rsqrt(spread + 1e-05)).reshape(2048, 128)
    out_w = out_w_ref[...]
    for s in range(16):
        update = dot(norm_buf[pl.ds(s, 128, stride=16), :].astype(BF16), out_w, 0, 0)
        for half in range(2):
            i = half * 16 + s
            at = pl.ds(i * 64, 64)
            out_ref[i] = (x_buf[at, :] + gate_buf[at, :] * update[half * 64 : (half + 1) * 64]).astype(BF16)
    all_to_all_sent(*edges)
    all_to_all_sent(*products)


def triangle(mask, cols, mix, output, left, right, gate_w, out_w):
    return pl.pallas_call(
        triangle_kernel,
        out_shape=jax.ShapeDtypeStruct((32, 64, 128), BF16),
        in_specs=[smem()] + [vmem()] * 7,
        out_specs=vmem(),
        scratch_shapes=[
            pltpu.VMEM((2048, 128), F32),
            pltpu.VMEM((128, 32, 128), BF16),
            pltpu.VMEM((16, 128, 128), BF16),
            pltpu.VMEM((128, 32, 128), BF16),
            pltpu.VMEM((16, 128, 128), BF16),
            pltpu.VMEM((4096, 128), F32),
            pltpu.VMEM((128, 16, 128), BF16),
            pltpu.VMEM((128, 16, 128), BF16),
            pltpu.VMEM((2048, 128), F32),
            pltpu.VMEM((2048, 128), F32),
            pltpu.VMEM((2048, 128), F32),
        ]
        + [pltpu.SemaphoreType.DMA] * 9
        + EVERYONE,
        compiler_params=pltpu.CompilerParams(
            collective_id=2, has_side_effects=True, vmem_limit_bytes=VMEM_LIMIT
        ),
        name="triangle",
    )(mask, cols, mix, output, left, right, gate_w, out_w)


def shards(
    pair_rep,
    tile_mask,
    chain_ids,
    chain_bias,
    row_project,
    row_bias_proj,
    row_output,
    col_project,
    col_bias_proj,
    col_output,
    tri_left,
    tri_right,
    tri_gate,
    tri_output,
):
    ids = chain_ids.reshape(1, 512)
    row_w, col_w = row_bias_proj.T, col_bias_proj.T
    g, *projected, steps, mask, add, ids = start(pair_rep, row_w, row_project, tile_mask, chain_bias, ids)
    mix = attention(0, mask, add, g, ids, steps, projected)
    g, *projected, steps, cols = middle(pair_rep, mix, row_output, col_w, col_project)
    mix = attention(1, mask, add, g, ids, steps, projected)
    return triangle(mask, cols, mix, col_output, tri_left, tri_right, tri_gate, tri_output)


def solution(mesh):
    spec = P(("row", "col"), None, None)
    return jax.shard_map(
        shards,
        mesh=mesh,
        in_specs=(spec,) + (P(),) * 13,
        out_specs=P("row", "col", None),
        check_vma=False,
    )
```

```python
import functools
import math

import jax
import jax.numpy as jnp
from jax import lax
from jax.experimental import pallas as pl
from jax.experimental.pallas import tpu as pltpu
from jax.sharding import PartitionSpec as P

MESH = pl.DeviceIdType.MESH
F32 = jnp.float32
BF16 = jnp.bfloat16
DEVS = 128
LOG2E = 1.4426950408889634
VMEM_LIMIT = 24 * 2**20


def cost(microseconds):
    return pl.CostEstimate(flops=int(microseconds * 1.1e9), bytes_accessed=4 * 2**20, transcendentals=0)


def vmem():
    return pl.BlockSpec(memory_space=pltpu.VMEM)


def smem():
    return pl.BlockSpec(memory_space=pltpu.SMEM)


def layer_norm(values):
    center = values - jnp.mean(values, axis=-1, keepdims=True)
    spread = jnp.mean(center * center, axis=-1, keepdims=True)
    return center * lax.rsqrt(spread + 1e-05)


def dot(a, b, ca=1, cb=0):
    return lax.dot_general(a, b, (((ca,), (cb,)), ((), ())), preferred_element_type=F32)


def sigmoid(x):
    return 1.0 / (1.0 + jnp.exp(-x))


def my_place():
    row, col = lax.axis_index("row"), lax.axis_index("col")
    return row, col, row * 8 + col


def at_offset(offset):
    row, col, _ = my_place()
    x = lax.rem(row // 4 + offset // 32, 4)
    y = lax.rem(row % 4 + offset // 8 % 4, 4)
    z = lax.rem(col // 2 + offset // 2 % 4, 4)
    return ((x * 4 + y) * 4 + z) * 2 + lax.rem(col % 2 + offset % 2, 2)


def drain(ref, sem):
    pltpu.make_async_copy(ref, ref, sem).wait()


def bias_step(w_ref):
    w = w_ref[...].astype(F32)
    length = jnp.sqrt(jnp.sum(w * w, axis=1, keepdims=True))
    return jnp.maximum(length, 1e-20) * (11.4 / 32766.0)


def code_bias(blk32, line, w_ref, inverse, normed):
    coded = jnp.round(dot(w_ref[...], normed, 1, 1) * inverse).astype(jnp.int32)
    for tile in range(4):
        blk32[tile // 2, tile % 2, line * 4 : line * 4 + 4, :] = coded[:, tile * 128 : (tile + 1) * 128]


def signal_partners():
    row, col, _ = my_place()
    core, z, y, x = col % 2, col // 2, row % 4, row // 4
    partners = []
    for step in range(4):
        for flip in range(2):
            if step or flip:
                partners.append((row, lax.rem(z + step, 4) * 2 + lax.rem(core + flip, 2)))
    for step in (1, 2, 3):
        partners.append((x * 4 + lax.rem(y + step, 4), col))
        partners.append((lax.rem(x + step, 4) * 4 + y, col))
    barrier = pltpu.get_barrier_semaphore()
    for partner in partners:
        pl.semaphore_signal(barrier, inc=1, device_id=partner, device_id_type=MESH)
    return len(partners)


class Everyone:
    def __init__(self, second, third):
        self.second, self.third = second, third
        self.count = signal_partners()

    def next_round(self):
        row, col, _ = my_place()
        x, y = row // 4, row % 4
        await_signals(self.count)
        for step in (1, 2, 3):
            for to in (x * 4 + lax.rem(y + step, 4), lax.rem(x + step, 4) * 4 + y):
                pl.semaphore_signal(self.second, inc=1, device_id=(to, col), device_id_type=MESH)

    def last_round(self):
        row, col, _ = my_place()
        pl.semaphore_wait(self.second, 6)
        for step in range(1, 8):
            pl.semaphore_signal(self.third, inc=1, device_id=(row, lax.rem(col + step, 8)), device_id_type=MESH)

    def wait(self):
        pl.semaphore_wait(self.third, 7)


EVERYONE = [pltpu.SemaphoreType.REGULAR] * 2


def await_signals(count):
    pl.semaphore_wait(pltpu.get_barrier_semaphore(), count)


G_SHAPE = (2, 128, 2, 16, 128)
GATHER_SEMS = [pltpu.SemaphoreType.DMA] * 3 + [pltpu.SemaphoreType.DMA((16,))] * 4


def near_row(half, offset):
    row, _, _ = my_place()
    y, x = row % 4, row // 4
    return jnp.where(half == 0, x * 4 + lax.rem(y + offset, 4), lax.rem(x + offset, 4) * 4 + y)


def far_row(half, offset):
    return near_row(1 - half, offset)


def signal_near():
    row, col, _ = my_place()
    core, z = col % 2, col // 2
    barrier = pltpu.get_barrier_semaphore()

    def step(i, carry):
        place = lax.rem(z + i // 2 % 4, 4) * 2 + lax.rem(core + i, 2)
        pl.semaphore_signal(barrier, inc=1, device_id=(near_row(core, i // 8), place), device_id_type=MESH)
        return carry

    lax.fori_loop(1, 32, step, 0)
    for offset in (1, 2, 3):
        pl.semaphore_signal(barrier, inc=1, device_id=(far_row(core, offset), col), device_id_type=MESH)
    return 34


def gather_bias(blk_ref, g_ref, own_sem, ns, nr, bs, br, fs, fr, work=()):
    row, col, dev = my_place()
    core, z, y, x = col % 2, col // 2, row % 4, row // 4
    sibling = (row, z * 2 + 1 - core)
    work = list(work)

    def do_work():
        if work:
            work.pop(0)()

    def part(half, start, size):
        return g_ref.at[half, pl.ds(start, size)]

    started = []

    def send(src, dst, ssem, rsem, device):
        copy = pltpu.make_async_remote_copy(
            src_ref=src, dst_ref=dst, send_sem=ssem, recv_sem=rsem, device_id=device, device_id_type=MESH
        )
        copy.start()
        started.append(copy)

    def send_near(half):
        def step(i, carry):
            to = lax.rem(i * 5, 16)
            pltpu.make_async_remote_copy(
                src_ref=blk_ref.at[pl.ds(half, 1)],
                dst_ref=g_ref.at[pl.ds(half, 1), dev],
                send_sem=ns,
                recv_sem=nr,
                device_id=(near_row(half, to // 4), lax.rem(z + to, 4) * 2 + half),
                device_id_type=MESH,
            ).start()
            return carry

        return step

    lax.fori_loop(1, 16, send_near(core), 0)
    lax.fori_loop(0, 16, send_near(1 - core), 0)
    own = pltpu.make_async_copy(blk_ref.at[pl.ds(core, 1)], g_ref.at[pl.ds(core, 1), dev], own_sem)
    own.start()
    do_work()
    own.wait()
    drain(g_ref.at[0, pl.ds(0, 31)], nr)

    def row_of(da, db):
        dx, dy = jnp.where(core == 0, db, da), jnp.where(core == 0, da, db)
        return lax.rem(x + dx, 4) * 4 + lax.rem(y + dy, 4)

    def block(da, db):
        return part(core, row_of(da, db) * 8, 8)

    def to_sibling(da, db):
        ref = block(da, db)
        send(ref, ref, fs.at[da * 4 + db], fr.at[da * 4 + db], sibling)

    for step in (1, 3, 2):
        for da in range(4):
            ref = block(da, 0)
            rel = 4 - step
            send(ref, ref, bs.at[da * 4 + rel], br.at[da * 4 + rel], (row_of(0, step), col))
    for da in range(4):
        to_sibling(da, 0)
    do_work()
    for db in (3, 1, 2):
        for da in range(4):
            drain(block(da, db), br.at[da * 4 + db])
            to_sibling(da, db)
    while work:
        do_work()
    for db in (0, 3, 1, 2):
        for da in range(4):
            drain(part(1 - core, row_of(db, da) * 8, 8), fr.at[da * 4 + db])
    for copy in started:
        copy.wait_send()
    drain(g_ref.at[0, pl.ds(0, 31)], ns)


PROJECTED = (
    jax.ShapeDtypeStruct((4, 512, 128), BF16),
    jax.ShapeDtypeStruct((4, 128, 512), BF16),
    jax.ShapeDtypeStruct((4, 128, 512), BF16),
    jax.ShapeDtypeStruct((4, 128, 512), F32),
)


def project_line(line, normed, project_ref, k_ref, q_ref, v_ref, gate_ref):
    k_ref[line] = dot(normed, project_ref[:, 128:256]).astype(BF16)
    q_ref[line] = dot(project_ref[:, 0:128], normed, 0, 1).astype(BF16)
    both = dot(project_ref[:, 256:512], normed, 0, 1)
    v_ref[line] = both[:128].astype(BF16)
    gate_ref[line] = sigmoid(both[128:])


BLK = [pltpu.VMEM((2, 2, 16, 128), jnp.int32), pltpu.VMEM((2, 2, 16, 128), jnp.int16)]
STEPS = jax.ShapeDtypeStruct((4, 128), F32)


def first_kernel(out_ref):
    out_ref[...] = jnp.zeros((8, 128), F32)


def first():
    return pl.pallas_call(
        first_kernel,
        out_shape=pltpu.VMEM((8, 128), F32),
        out_specs=vmem(),
        cost_estimate=cost(6),
        name="first",
    )()


def start_kernel(
    first_ref,
    x_ref,
    bias_w_ref,
    project_ref,
    g_ref,
    k_ref,
    q_ref,
    v_ref,
    gate_ref,
    steps_ref,
    blk32,
    blk,
    normed_buf,
    *sems,
):
    signals = signal_near()
    step = bias_step(bias_w_ref)
    steps_ref[...] = jnp.broadcast_to(step, (4, 128))
    inverse = 1.0 / step
    for line in range(4):
        normed = layer_norm(x_ref[line].astype(F32)).astype(BF16)
        normed_buf[line] = normed
        code_bias(blk32, line, bias_w_ref, inverse, normed)
    blk[...] = blk32[...].astype(jnp.int16)
    await_signals(signals)

    def work(lines):
        for line in lines:
            project_line(line, normed_buf[line], project_ref, k_ref, q_ref, v_ref, gate_ref)

    gather_bias(blk, g_ref, *sems, work=[functools.partial(work, lines) for lines in ((0, 1), (2, 3))])


def start(x, bias_w, project):
    return pl.pallas_call(
        start_kernel,
        out_shape=(jax.ShapeDtypeStruct(G_SHAPE, jnp.int16),) + PROJECTED + (STEPS,),
        in_specs=[vmem()] * 4,
        out_specs=(vmem(),) * 6,
        scratch_shapes=BLK + [pltpu.VMEM((4, 512, 128), BF16)] + GATHER_SEMS,
        compiler_params=pltpu.CompilerParams(
            collective_id=0, has_side_effects=True, vmem_limit_bytes=VMEM_LIMIT
        ),
        cost_estimate=cost(20),
        name="bias_gather",
    )(first(), x, bias_w, project)


def all_to_all_some(src_ref, dst_ref, ssem, rsem, lsem, first, last):
    row, col, dev = my_place()

    def step(i, carry):
        dest = at_offset(lax.rem(i * 37, DEVS))
        pltpu.make_async_remote_copy(
            src_ref=src_ref.at[dest],
            dst_ref=dst_ref.at[dev],
            send_sem=ssem,
            recv_sem=rsem,
            device_id=(dest // 8, dest % 8),
            device_id_type=MESH,
        ).start()
        return carry

    if first == 1:
        pltpu.make_async_copy(src_ref.at[dev], dst_ref.at[dev], lsem).start()
    lax.fori_loop(first, last, step, 0)


def all_to_all_start(*args):
    all_to_all_some(*args, 1, DEVS)


def all_to_all_recv(src_ref, dst_ref, ssem, rsem, lsem):
    drain(dst_ref.at[0], lsem)
    drain(dst_ref.at[pl.ds(0, DEVS - 1)], rsem)


def all_to_all_sent(src_ref, dst_ref, ssem, rsem, lsem):
    drain(src_ref.at[pl.ds(0, DEVS - 1)], ssem)


def middle_kernel(
    x_ref,
    mix_ref,
    output_ref,
    bias_w_ref,
    project_ref,
    g_ref,
    k_ref,
    q_ref,
    v_ref,
    gate_ref,
    steps_ref,
    cols_ref,
    line_buf,
    send_buf,
    tiles,
    cols_buf,
    blk32,
    blk,
    second_round,
    third_round,
    s0,
    s1,
    s2,
    *sems,
):
    everyone = Everyone(second_round, third_round)
    step = bias_step(bias_w_ref)
    steps_ref[...] = jnp.broadcast_to(step, (4, 128))
    inverse = 1.0 / step
    w_o = output_ref[...]
    for line in range(4):
        value = x_ref[line].astype(F32) + dot(mix_ref[line], w_o, 0, 0)
        value = value.astype(BF16).astype(F32)
        code_bias(blk32, line, bias_w_ref, inverse, layer_norm(value).astype(BF16))
        line_buf[line] = value
        for j in range(4):
            send_buf[pl.ds(line * 4 + j, 128, stride=16), :] = line_buf[line, pl.ds(j, 128, stride=4), :]
        if line == 1:
            everyone.next_round()
        if line == 3:
            everyone.last_round()
    blk[...] = blk32[...].astype(jnp.int16)
    tiles[...] = send_buf[...].reshape(128, 16, 128).astype(BF16)
    everyone.wait()
    args = (tiles, cols_ref, s0, s1, s2)

    def project_all():
        all_to_all_recv(*args)
        cols_buf[...] = cols_ref[...].astype(F32).reshape(2048, 128)
        for line in range(4):
            normed = layer_norm(cols_buf[pl.ds(line, 512, stride=4), :]).astype(BF16)
            project_line(line, normed, project_ref, k_ref, q_ref, v_ref, gate_ref)

    work = [functools.partial(all_to_all_some, *args, lo, hi) for lo, hi in ((1, 65), (65, 128))]
    gather_bias(blk, g_ref, *sems, work=work + [project_all])
    all_to_all_sent(*args)


def middle(x, mix, output, bias_w, project):
    return pl.pallas_call(
        middle_kernel,
        out_shape=(jax.ShapeDtypeStruct(G_SHAPE, jnp.int16),)
        + PROJECTED
        + (STEPS, jax.ShapeDtypeStruct((128, 16, 128), BF16)),
        in_specs=[vmem()] * 5,
        out_specs=(vmem(),) * 7,
        scratch_shapes=[
            pltpu.VMEM((4, 512, 128), F32),
            pltpu.VMEM((2048, 128), F32),
            pltpu.VMEM((128, 16, 128), BF16),
            pltpu.VMEM((2048, 128), F32),
        ]
        + BLK
        + EVERYONE
        + [pltpu.SemaphoreType.DMA] * 3
        + GATHER_SEMS,
        compiler_params=pltpu.CompilerParams(
            collective_id=1, has_side_effects=True, vmem_limit_bytes=VMEM_LIMIT
        ),
        cost_estimate=cost(28),
        name="columns_and_bias",
    )(x, mix, output, bias_w, project)


def compact(flags):
    count = jnp.int32(0)
    picked = [jnp.int32(0)] * 4
    for tile in range(4):
        for place in range(4):
            hit = jnp.logical_and(flags[tile] > 0, count == place)
            picked[place] = jnp.where(hit, tile, picked[place])
        count = count + flags[tile]
    return picked, count


def attention_kernel(
    which, mask_ref, add_ref, g_ref, ids_ref, steps_ref, k_ref, q_ref, v_ref, gate_ref, mix_ref, bias_buf, code_buf, ids_buf
):
    row, _, _ = my_place()
    flags = [mask_ref[row // 4, t] if which == 0 else mask_ref[t, row // 4] for t in range(4)]
    scale = LOG2E * 32 ** (-0.5)
    ids = ids_ref[...].astype(F32)
    for tile in range(4):
        ids_buf[tile] = jnp.broadcast_to(ids[:, tile * 128 : (tile + 1) * 128], (128, 128)).T
    picked, count = compact(flags)
    steps = steps_ref[...] * LOG2E
    adds = [add_ref[which, head] * LOG2E for head in range(4)]
    lanes = lax.broadcasted_iota(jnp.int32, (1, 128), 1) // 32
    head_masks = [jnp.where(lanes == head, 1.0, 0.0).astype(BF16) for head in range(4)]
    upper = lax.broadcasted_iota(jnp.int32, (64, 128), 0) < 32

    def run(tiles):
        def load_bias(place):
            tile = picked[place]
            if which == 0:
                code_buf[...] = g_ref[tile // 2, :, tile % 2].astype(F32).reshape(2048, 128)
            for q_tile in range(4):
                if which == 1:
                    got = g_ref[q_tile // 2, pl.ds(tile * 32, 32), q_tile % 2].astype(F32)
                    code_buf[0:512, :] = got.reshape(512, 128)
                same = ids_buf[tile] == ids[:, q_tile * 128 : (q_tile + 1) * 128]
                for head in range(4):
                    if which == 0:
                        code = code_buf[pl.ds(q_tile * 512 + head, 128, stride=4), :].T
                    else:
                        code = code_buf[pl.ds(head, 128, stride=4), :]
                    bias = code * steps[head : head + 1] + jnp.where(same, adds[head], 0.0)
                    bias_buf[head, place, :, q_tile * 128 : (q_tile + 1) * 128] = bias

        for place in range(tiles):
            load_bias(place)

        def body(step, carry):
            line, block = step // 2, step % 2
            q_at = pl.ds(pl.multiple_of(block * 256, 256), 256)
            q = q_ref[line, :, q_at]
            k_at = [pl.ds(pl.multiple_of(picked[place] * 128, 128), 128) for place in range(tiles)]
            scores = []
            for place in range(tiles):
                keys = k_ref[line, k_at[place], :]
                stacked = jnp.concatenate([keys * head_masks[head] for head in range(4)], axis=0)
                scores.append(dot(stacked, q))
            for pair in range(2):
                weights, totals = [], []
                for head in (2 * pair, 2 * pair + 1):
                    logits = [
                        scores[place][head * 128 : (head + 1) * 128] * scale + bias_buf[head, place, :, q_at]
                        for place in range(tiles)
                    ]
                    peak = functools.reduce(jnp.maximum, [jnp.max(s, axis=0, keepdims=True) for s in logits])
                    own = [jnp.exp2(s - peak) for s in logits]
                    totals.append(functools.reduce(jnp.add, [jnp.sum(w, axis=0, keepdims=True) for w in own]))
                    weights.append([w.astype(BF16) for w in own])
                rows = pl.ds(64 * pair, 64)
                mixed = None
                for place in range(tiles):
                    v = v_ref[line, rows, k_at[place]]
                    zero = jnp.zeros_like(v)
                    spread = jnp.concatenate([jnp.where(upper, v, zero), jnp.where(upper, zero, v)], axis=1)
                    term = dot(spread, jnp.concatenate([weights[0][place], weights[1][place]], axis=0))
                    mixed = term if mixed is None else mixed + term
                inverse = [1.0 / total for total in totals]
                for sub in range(2):
                    at = pl.ds(64 * pair + 32 * sub, 32)
                    gated = mixed[32 * sub : 32 * sub + 32] * inverse[sub] * gate_ref[line, at, q_at]
                    mix_ref[line, at, q_at] = gated.astype(BF16)
            return carry

        lax.fori_loop(0, 8, body, 0)

    for tiles in range(1, 5):
        pl.when(count == tiles)(functools.partial(run, tiles))


def attention(which, mask, add, g, ids, steps, projected):
    return pl.pallas_call(
        functools.partial(attention_kernel, which),
        out_shape=jax.ShapeDtypeStruct((4, 128, 512), BF16),
        in_specs=[smem(), smem()] + [vmem()] * 7,
        out_specs=vmem(),
        scratch_shapes=[
            pltpu.VMEM((4, 4, 128, 512), F32),
            pltpu.VMEM((2048, 128), F32),
            pltpu.VMEM((4, 128, 128), F32),
        ],
        compiler_params=pltpu.CompilerParams(vmem_limit_bytes=VMEM_LIMIT),
        cost_estimate=cost(6),
        name=("row_attention", "col_attention")[which],
    )(mask, add, g, ids, steps, *projected)


def triangle_kernel(
    mask_ref,
    cols_ref,
    mix_ref,
    output_ref,
    left_ref,
    right_ref,
    gate_w_ref,
    out_w_ref,
    out_ref,
    cols_buf,
    edge_ref,
    second_ref,
    edge_in,
    second_in,
    edge_buf,
    prod_send,
    prod_in,
    x_buf,
    gate_buf,
    norm_buf,
    es,
    er,
    el,
    ss,
    sr,
    sl,
    ps,
    pr,
    pl_,
    second_round,
    third_round,
):
    row, col, dev = my_place()
    everyone = Everyone(second_round, third_round)
    flags = [mask_ref[tile, row // 4].astype(F32) for tile in range(4)]
    cols_buf[...] = cols_ref[...].astype(F32).reshape(2048, 128)
    w_o = output_ref[...]
    for line in range(4):
        value = cols_buf[pl.ds(line, 512, stride=4), :] + dot(mix_ref[line], w_o, 0, 0)
        rounded = value.astype(BF16)
        second_ref[:, line * 32 : (line + 1) * 32, :] = rounded.reshape(16, 32, 128)
        normed = layer_norm(rounded.astype(F32)).astype(BF16)
        for side, w_ref in enumerate((left_ref, right_ref)):
            both = dot(w_ref[...], normed, 0, 1)
            act = sigmoid(both[128:]) * both[:128]
            for tile in range(4):
                edge_buf[pl.ds(line * 8 + side * 4 + tile, 128, stride=32), :] = (
                    act[:, tile * 128 : (tile + 1) * 128] * flags[tile]
                )
        if line == 1:
            everyone.next_round()
        if line == 3:
            everyone.last_round()
    edge_ref[...] = edge_buf[...].reshape(128, 32, 128).astype(BF16)
    everyone.wait()
    edges = (edge_ref, edge_in, es, er, el)
    all_to_all_start(*edges)
    slot = lax.rem(dev, 16)
    grid_col = dev // 16

    def send_second(step, carry):
        to_row = lax.rem(row + step, 16)

        @pl.when(jnp.logical_and(to_row == row, grid_col == col))
        def _():
            pltpu.make_async_copy(second_ref.at[to_row], second_in.at[slot], sl).start()

        @pl.when(jnp.logical_not(jnp.logical_and(to_row == row, grid_col == col)))
        def _():
            pltpu.make_async_remote_copy(
                src_ref=second_ref.at[to_row],
                dst_ref=second_in.at[slot],
                send_sem=ss,
                recv_sem=sr,
                device_id=(to_row, grid_col),
                device_id_type=MESH,
            ).start()

        return carry

    all_to_all_recv(*edges)
    lax.fori_loop(0, 16, send_second, 0)
    edge_buf[...] = edge_in[...].astype(F32).reshape(4096, 128)
    right = jnp.concatenate([edge_buf[pl.ds(4 + tile, 512, stride=8), :] for tile in range(4)], axis=1).astype(BF16)
    low = lax.broadcasted_iota(jnp.int32, (16, 128), 1) < 64
    products = (prod_send, prod_in, ps, pr, pl_)

    def send_product(slab, first):
        def step(i, carry):
            dest = at_offset(slab * 32 + lax.rem(i * 13, 32))
            pltpu.make_async_remote_copy(
                src_ref=prod_send.at[dest],
                dst_ref=prod_in.at[dev],
                send_sem=ps,
                recv_sem=pr,
                device_id=(dest // 8, dest % 8),
                device_id_type=MESH,
            ).start()
            return carry

        lax.fori_loop(first, 32, step, 0)

    for slab in range(4):
        tile = lax.rem(row // 4 + slab, 4)
        left = edge_buf[pl.ds(tile, 512, stride=8), :].astype(BF16)
        product = dot(left, right, 0, 0)
        for sub in range(4):
            for t in range(4):
                a = product[sub * 32 : sub * 32 + 16, t * 128 : (t + 1) * 128]
                b = product[sub * 32 + 16 : sub * 32 + 32, t * 128 : (t + 1) * 128]
                block = tile * 32 + sub * 8 + 2 * t
                prod_send[block] = jnp.where(low, a, pltpu.roll(b, 64, 1)).astype(BF16)
                prod_send[block + 1] = jnp.where(low, pltpu.roll(a, 64, 1), b).astype(BF16)
        if slab == 0:
            pltpu.make_async_copy(prod_send.at[dev], prod_in.at[dev], pl_).start()
        send_product(slab, 1 if slab == 0 else 0)

    own_sent = grid_col == col

    @pl.when(own_sent)
    def _():
        drain(second_in.at[0], sl)
        drain(second_in.at[pl.ds(0, 15)], sr)
        drain(second_ref.at[pl.ds(0, 15)], ss)

    @pl.when(jnp.logical_not(own_sent))
    def _():
        drain(second_in, sr)
        drain(second_ref, ss)

    gate_w = gate_w_ref[...]

    def gates(j, carry):
        at = pl.multiple_of(j * 128, 128)
        x = second_in[j].astype(F32)
        gate = sigmoid(dot(layer_norm(x).astype(BF16), gate_w))
        for sub in range(4):
            x_buf[pl.ds(j * 4 + sub, 32, stride=64), :] = x[sub * 32 : (sub + 1) * 32]
            gate_buf[pl.ds(j * 4 + sub, 32, stride=64), :] = gate[sub * 32 : (sub + 1) * 32]
        return carry

    lax.fori_loop(0, 16, gates, 0)
    all_to_all_recv(*products)
    product = prod_in[...].astype(F32)
    center = product - jnp.mean(product, axis=0, keepdims=True)
    spread = jnp.mean(center * center, axis=0, keepdims=True)
    norm_buf[...] = (center * lax.rsqrt(spread + 1e-05)).reshape(2048, 128)
    out_w = out_w_ref[...]
    for s in range(16):
        update = dot(norm_buf[pl.ds(s, 128, stride=16), :].astype(BF16), out_w, 0, 0)
        for half in range(2):
            i = half * 16 + s
            at = pl.ds(i * 64, 64)
            out_ref[i] = (x_buf[at, :] + gate_buf[at, :] * update[half * 64 : (half + 1) * 64]).astype(BF16)
    all_to_all_sent(*edges)
    all_to_all_sent(*products)


def triangle(mask, cols, mix, output, left, right, gate_w, out_w):
    return pl.pallas_call(
        triangle_kernel,
        out_shape=jax.ShapeDtypeStruct((32, 64, 128), BF16),
        in_specs=[smem()] + [vmem()] * 7,
        out_specs=vmem(),
        scratch_shapes=[
            pltpu.VMEM((2048, 128), F32),
            pltpu.VMEM((128, 32, 128), BF16),
            pltpu.VMEM((16, 128, 128), BF16),
            pltpu.VMEM((128, 32, 128), BF16),
            pltpu.VMEM((16, 128, 128), BF16),
            pltpu.VMEM((4096, 128), F32),
            pltpu.VMEM((128, 16, 128), BF16),
            pltpu.VMEM((128, 16, 128), BF16),
            pltpu.VMEM((2048, 128), F32),
            pltpu.VMEM((2048, 128), F32),
            pltpu.VMEM((2048, 128), F32),
        ]
        + [pltpu.SemaphoreType.DMA] * 9
        + EVERYONE,
        compiler_params=pltpu.CompilerParams(
            collective_id=2, has_side_effects=True, vmem_limit_bytes=VMEM_LIMIT
        ),
        cost_estimate=cost(38),
        name="triangle",
    )(mask, cols, mix, output, left, right, gate_w, out_w)


def shards(
    pair_rep,
    tile_mask,
    chain_ids,
    chain_bias,
    row_project,
    row_bias_proj,
    row_output,
    col_project,
    col_bias_proj,
    col_output,
    tri_left,
    tri_right,
    tri_gate,
    tri_output,
):
    ids = chain_ids.reshape(1, 512)
    row_w, col_w = row_bias_proj.T, col_bias_proj.T
    mask, add = tile_mask, chain_bias
    g, *projected, steps = start(pair_rep, row_w, row_project)
    mix = attention(0, mask, add, g, ids, steps, projected)
    g, *projected, steps, cols = middle(pair_rep, mix, row_output, col_w, col_project)
    mix = attention(1, mask, add, g, ids, steps, projected)
    return triangle(mask, cols, mix, col_output, tri_left, tri_right, tri_gate, tri_output)


def solution(mesh):
    spec = P(("row", "col"), None, None)
    return jax.shard_map(
        shards,
        mesh=mesh,
        in_specs=(spec,) + (P(),) * 13,
        out_specs=P("row", "col", None),
        check_vma=False,
    )
```

```python
import functools
import math

import jax
import jax.numpy as jnp
from jax import lax
from jax.experimental import pallas as pl
from jax.experimental.pallas import tpu as pltpu
from jax.sharding import PartitionSpec as P

MESH = pl.DeviceIdType.MESH
F32 = jnp.float32
BF16 = jnp.bfloat16
DEVS = 128
LOG2E = 1.4426950408889634
VMEM_LIMIT = 24 * 2**20


def cost(microseconds):
    return pl.CostEstimate(flops=int(microseconds * 1.1e9), bytes_accessed=4 * 2**20, transcendentals=0)


def vmem():
    return pl.BlockSpec(memory_space=pltpu.VMEM)


def smem():
    return pl.BlockSpec(memory_space=pltpu.SMEM)


def layer_norm(values):
    center = values - jnp.mean(values, axis=-1, keepdims=True)
    spread = jnp.mean(center * center, axis=-1, keepdims=True)
    return center * lax.rsqrt(spread + 1e-05)


def dot(a, b, ca=1, cb=0):
    return lax.dot_general(a, b, (((ca,), (cb,)), ((), ())), preferred_element_type=F32)


def sigmoid(x):
    return 1.0 / (1.0 + jnp.exp(-x))


def my_place():
    row, col = lax.axis_index("row"), lax.axis_index("col")
    return row, col, row * 8 + col


def at_offset(offset):
    row, col, _ = my_place()
    x = lax.rem(row // 4 + offset // 32, 4)
    y = lax.rem(row % 4 + offset // 8 % 4, 4)
    z = lax.rem(col // 2 + offset // 2 % 4, 4)
    return ((x * 4 + y) * 4 + z) * 2 + lax.rem(col % 2 + offset % 2, 2)


def drain(ref, sem):
    pltpu.make_async_copy(ref, ref, sem).wait()


def bias_step(w_ref):
    w = w_ref[...].astype(F32)
    length = jnp.sqrt(jnp.sum(w * w, axis=1, keepdims=True))
    return jnp.maximum(length, 1e-20) * (11.4 / 32766.0)


def code_bias(blk32, line, w_ref, inverse, normed):
    coded = jnp.round(dot(w_ref[...], normed, 1, 1) * inverse).astype(jnp.int32)
    for tile in range(4):
        blk32[tile // 2, tile % 2, line * 4 : line * 4 + 4, :] = coded[:, tile * 128 : (tile + 1) * 128]


class Everyone:
    def __init__(self, second):
        self.second = second
        row, col, _ = my_place()
        x, y = row // 4, row % 4
        barrier = pltpu.get_barrier_semaphore()

        def step(i, carry):
            to = (x * 4 + lax.rem(y + i // 8, 4), lax.rem(col + i, 8))
            pl.semaphore_signal(barrier, inc=1, device_id=to, device_id_type=MESH)
            return carry

        lax.fori_loop(1, 32, step, 0)
        self.line = [(lax.rem(x + offset, 4) * 4 + y, col) for offset in (1, 2, 3)]
        for to in self.line:
            pl.semaphore_signal(barrier, inc=1, device_id=to, device_id_type=MESH)

    def next_round(self):
        await_signals(34)
        for to in self.line:
            pl.semaphore_signal(self.second, inc=1, device_id=to, device_id_type=MESH)

    def wait(self):
        pl.semaphore_wait(self.second, 3)


EVERYONE = [pltpu.SemaphoreType.REGULAR]


def await_signals(count):
    pl.semaphore_wait(pltpu.get_barrier_semaphore(), count)


G_SHAPE = (2, 128, 2, 16, 128)
GATHER_SEMS = [pltpu.SemaphoreType.DMA] * 3 + [pltpu.SemaphoreType.DMA((16,))] * 4


def near_row(half, offset):
    row, _, _ = my_place()
    y, x = row % 4, row // 4
    return jnp.where(half == 0, x * 4 + lax.rem(y + offset, 4), lax.rem(x + offset, 4) * 4 + y)


def far_row(half, offset):
    return near_row(1 - half, offset)


def signal_near():
    row, col, _ = my_place()
    core, z = col % 2, col // 2
    barrier = pltpu.get_barrier_semaphore()

    def step(i, carry):
        place = lax.rem(z + i // 2 % 4, 4) * 2 + lax.rem(core + i, 2)
        pl.semaphore_signal(barrier, inc=1, device_id=(near_row(core, i // 8), place), device_id_type=MESH)
        return carry

    lax.fori_loop(1, 32, step, 0)
    for offset in (1, 2, 3):
        pl.semaphore_signal(barrier, inc=1, device_id=(far_row(core, offset), col), device_id_type=MESH)
    return 34


def gather_bias(blk_ref, g_ref, own_sem, ns, nr, bs, br, fs, fr, work=()):
    row, col, dev = my_place()
    core, z, y, x = col % 2, col // 2, row % 4, row // 4
    sibling = (row, z * 2 + 1 - core)
    work = list(work)

    def do_work():
        if work:
            work.pop(0)()

    def part(half, start, size):
        return g_ref.at[half, pl.ds(start, size)]

    started = []

    def send(src, dst, ssem, rsem, device):
        copy = pltpu.make_async_remote_copy(
            src_ref=src, dst_ref=dst, send_sem=ssem, recv_sem=rsem, device_id=device, device_id_type=MESH
        )
        copy.start()
        started.append(copy)

    def send_near(half):
        def step(i, carry):
            to = lax.rem(i * 5, 16)
            pltpu.make_async_remote_copy(
                src_ref=blk_ref.at[pl.ds(half, 1)],
                dst_ref=g_ref.at[pl.ds(half, 1), dev],
                send_sem=ns,
                recv_sem=nr,
                device_id=(near_row(half, to // 4), lax.rem(z + to, 4) * 2 + half),
                device_id_type=MESH,
            ).start()
            return carry

        return step

    lax.fori_loop(1, 16, send_near(core), 0)
    lax.fori_loop(0, 16, send_near(1 - core), 0)
    own = pltpu.make_async_copy(blk_ref.at[pl.ds(core, 1)], g_ref.at[pl.ds(core, 1), dev], own_sem)
    own.start()
    do_work()
    own.wait()
    drain(g_ref.at[0, pl.ds(0, 31)], nr)

    def row_of(da, db):
        dx, dy = jnp.where(core == 0, db, da), jnp.where(core == 0, da, db)
        return lax.rem(x + dx, 4) * 4 + lax.rem(y + dy, 4)

    def block(da, db):
        return part(core, row_of(da, db) * 8, 8)

    def to_sibling(da, db):
        ref = block(da, db)
        send(ref, ref, fs.at[da * 4 + db], fr.at[da * 4 + db], sibling)

    for step in (1, 3, 2):
        for da in range(4):
            ref = block(da, 0)
            rel = 4 - step
            send(ref, ref, bs.at[da * 4 + rel], br.at[da * 4 + rel], (row_of(0, step), col))
    for da in range(4):
        to_sibling(da, 0)
    do_work()
    for db in (3, 1, 2):
        for da in range(4):
            drain(block(da, db), br.at[da * 4 + db])
            to_sibling(da, db)
    while work:
        do_work()
    for db in (0, 3, 1, 2):
        for da in range(4):
            drain(part(1 - core, row_of(db, da) * 8, 8), fr.at[da * 4 + db])
    for copy in started:
        copy.wait_send()
    drain(g_ref.at[0, pl.ds(0, 31)], ns)


PROJECTED = (
    jax.ShapeDtypeStruct((4, 512, 128), BF16),
    jax.ShapeDtypeStruct((4, 128, 512), BF16),
    jax.ShapeDtypeStruct((4, 128, 512), BF16),
    jax.ShapeDtypeStruct((4, 128, 512), F32),
)


def project_line(line, normed, project_ref, k_ref, q_ref, v_ref, gate_ref):
    k_ref[line] = dot(normed, project_ref[:, 128:256]).astype(BF16)
    q_ref[line] = dot(project_ref[:, 0:128], normed, 0, 1).astype(BF16)
    both = dot(project_ref[:, 256:512], normed, 0, 1)
    v_ref[line] = both[:128].astype(BF16)
    gate_ref[line] = sigmoid(both[128:])


BLK = [pltpu.VMEM((2, 2, 16, 128), jnp.int32), pltpu.VMEM((2, 2, 16, 128), jnp.int16)]
STEPS = jax.ShapeDtypeStruct((4, 128), F32)


def first_kernel(out_ref):
    out_ref[...] = jnp.zeros((8, 128), F32)


def first():
    return pl.pallas_call(
        first_kernel,
        out_shape=pltpu.VMEM((8, 128), F32),
        out_specs=vmem(),
        cost_estimate=cost(6),
        name="first",
    )()


def start_kernel(
    first_ref,
    x_ref,
    bias_w_ref,
    project_ref,
    g_ref,
    k_ref,
    q_ref,
    v_ref,
    gate_ref,
    steps_ref,
    blk32,
    blk,
    normed_buf,
    *sems,
):
    signals = signal_near()
    step = bias_step(bias_w_ref)
    steps_ref[...] = jnp.broadcast_to(step, (4, 128))
    inverse = 1.0 / step
    for line in range(4):
        normed = layer_norm(x_ref[line].astype(F32)).astype(BF16)
        normed_buf[line] = normed
        code_bias(blk32, line, bias_w_ref, inverse, normed)
    blk[...] = blk32[...].astype(jnp.int16)
    await_signals(signals)

    def work(lines):
        for line in lines:
            project_line(line, normed_buf[line], project_ref, k_ref, q_ref, v_ref, gate_ref)

    gather_bias(blk, g_ref, *sems, work=[functools.partial(work, lines) for lines in ((0, 1), (2, 3))])


def start(x, bias_w, project):
    return pl.pallas_call(
        start_kernel,
        out_shape=(jax.ShapeDtypeStruct(G_SHAPE, jnp.int16),) + PROJECTED + (STEPS,),
        in_specs=[vmem()] * 4,
        out_specs=(vmem(),) * 6,
        scratch_shapes=BLK + [pltpu.VMEM((4, 512, 128), BF16)] + GATHER_SEMS,
        compiler_params=pltpu.CompilerParams(
            collective_id=0, has_side_effects=True, vmem_limit_bytes=VMEM_LIMIT
        ),
        cost_estimate=cost(20),
        name="bias_gather",
    )(first(), x, bias_w, project)


def all_to_all_some(src_ref, dst_ref, ssem, rsem, lsem, first, last):
    row, col, dev = my_place()

    def step(i, carry):
        dest = at_offset(lax.rem(i * 37, DEVS))
        pltpu.make_async_remote_copy(
            src_ref=src_ref.at[dest],
            dst_ref=dst_ref.at[dev],
            send_sem=ssem,
            recv_sem=rsem,
            device_id=(dest // 8, dest % 8),
            device_id_type=MESH,
        ).start()
        return carry

    if first == 1:
        pltpu.make_async_copy(src_ref.at[dev], dst_ref.at[dev], lsem).start()
    lax.fori_loop(first, last, step, 0)


def all_to_all_start(*args):
    all_to_all_some(*args, 1, DEVS)


def all_to_all_recv(src_ref, dst_ref, ssem, rsem, lsem):
    drain(dst_ref.at[0], lsem)
    drain(dst_ref.at[pl.ds(0, DEVS - 1)], rsem)


def all_to_all_sent(src_ref, dst_ref, ssem, rsem, lsem):
    drain(src_ref.at[pl.ds(0, DEVS - 1)], ssem)


def middle_kernel(
    x_ref,
    mix_ref,
    output_ref,
    bias_w_ref,
    project_ref,
    g_ref,
    k_ref,
    q_ref,
    v_ref,
    gate_ref,
    steps_ref,
    cols_ref,
    line_buf,
    send_buf,
    tiles,
    cols_buf,
    blk32,
    blk,
    second_round,
    s0,
    s1,
    s2,
    *sems,
):
    everyone = Everyone(second_round)
    step = bias_step(bias_w_ref)
    steps_ref[...] = jnp.broadcast_to(step, (4, 128))
    inverse = 1.0 / step
    w_o = output_ref[...]
    for line in range(4):
        value = x_ref[line].astype(F32) + dot(mix_ref[line], w_o, 0, 0)
        value = value.astype(BF16).astype(F32)
        code_bias(blk32, line, bias_w_ref, inverse, layer_norm(value).astype(BF16))
        line_buf[line] = value
        for j in range(4):
            send_buf[pl.ds(line * 4 + j, 128, stride=16), :] = line_buf[line, pl.ds(j, 128, stride=4), :]
        if line == 2:
            everyone.next_round()
    blk[...] = blk32[...].astype(jnp.int16)
    tiles[...] = send_buf[...].reshape(128, 16, 128).astype(BF16)
    everyone.wait()
    args = (tiles, cols_ref, s0, s1, s2)

    def project_all():
        all_to_all_recv(*args)
        cols_buf[...] = cols_ref[...].astype(F32).reshape(2048, 128)
        for line in range(4):
            normed = layer_norm(cols_buf[pl.ds(line, 512, stride=4), :]).astype(BF16)
            project_line(line, normed, project_ref, k_ref, q_ref, v_ref, gate_ref)

    gather_bias(blk, g_ref, *sems, work=[functools.partial(all_to_all_start, *args), project_all])
    all_to_all_sent(*args)


def middle(x, mix, output, bias_w, project):
    return pl.pallas_call(
        middle_kernel,
        out_shape=(jax.ShapeDtypeStruct(G_SHAPE, jnp.int16),)
        + PROJECTED
        + (STEPS, jax.ShapeDtypeStruct((128, 16, 128), BF16)),
        in_specs=[vmem()] * 5,
        out_specs=(vmem(),) * 7,
        scratch_shapes=[
            pltpu.VMEM((4, 512, 128), F32),
            pltpu.VMEM((2048, 128), F32),
            pltpu.VMEM((128, 16, 128), BF16),
            pltpu.VMEM((2048, 128), F32),
        ]
        + BLK
        + EVERYONE
        + [pltpu.SemaphoreType.DMA] * 3
        + GATHER_SEMS,
        compiler_params=pltpu.CompilerParams(
            collective_id=1, has_side_effects=True, vmem_limit_bytes=VMEM_LIMIT
        ),
        cost_estimate=cost(28),
        name="columns_and_bias",
    )(x, mix, output, bias_w, project)


def compact(flags):
    count = jnp.int32(0)
    picked = [jnp.int32(0)] * 4
    for tile in range(4):
        for place in range(4):
            hit = jnp.logical_and(flags[tile] > 0, count == place)
            picked[place] = jnp.where(hit, tile, picked[place])
        count = count + flags[tile]
    return picked, count


def attention_kernel(
    which, mask_ref, add_ref, g_ref, ids_ref, steps_ref, k_ref, q_ref, v_ref, gate_ref, mix_ref, bias_buf, code_buf, ids_buf
):
    row, _, _ = my_place()
    flags = [mask_ref[row // 4, t] if which == 0 else mask_ref[t, row // 4] for t in range(4)]
    scale = LOG2E * 32 ** (-0.5)
    ids = ids_ref[...].astype(F32)
    for tile in range(4):
        ids_buf[tile] = jnp.broadcast_to(ids[:, tile * 128 : (tile + 1) * 128], (128, 128)).T
    picked, count = compact(flags)
    steps = steps_ref[...] * LOG2E
    adds = [add_ref[which, head] * LOG2E for head in range(4)]
    lanes = lax.broadcasted_iota(jnp.int32, (1, 128), 1) // 32
    head_masks = [jnp.where(lanes == head, 1.0, 0.0).astype(BF16) for head in range(4)]
    upper = lax.broadcasted_iota(jnp.int32, (64, 128), 0) < 32

    def run(tiles):
        def load_bias(place):
            tile = picked[place]
            if which == 0:
                code_buf[...] = g_ref[tile // 2, :, tile % 2].astype(F32).reshape(2048, 128)
            for q_tile in range(4):
                if which == 1:
                    got = g_ref[q_tile // 2, pl.ds(tile * 32, 32), q_tile % 2].astype(F32)
                    code_buf[0:512, :] = got.reshape(512, 128)
                same = ids_buf[tile] == ids[:, q_tile * 128 : (q_tile + 1) * 128]
                for head in range(4):
                    if which == 0:
                        code = code_buf[pl.ds(q_tile * 512 + head, 128, stride=4), :].T
                    else:
                        code = code_buf[pl.ds(head, 128, stride=4), :]
                    bias = code * steps[head : head + 1] + jnp.where(same, adds[head], 0.0)
                    bias_buf[head, place, :, q_tile * 128 : (q_tile + 1) * 128] = bias

        for place in range(tiles):
            load_bias(place)

        def body(step, carry):
            line, block = step // 2, step % 2
            q_at = pl.ds(pl.multiple_of(block * 256, 256), 256)
            q = q_ref[line, :, q_at]
            k_at = [pl.ds(pl.multiple_of(picked[place] * 128, 128), 128) for place in range(tiles)]
            scores = []
            for place in range(tiles):
                keys = k_ref[line, k_at[place], :]
                stacked = jnp.concatenate([keys * head_masks[head] for head in range(4)], axis=0)
                scores.append(dot(stacked, q))
            for pair in range(2):
                weights, totals = [], []
                for head in (2 * pair, 2 * pair + 1):
                    logits = [
                        scores[place][head * 128 : (head + 1) * 128] * scale + bias_buf[head, place, :, q_at]
                        for place in range(tiles)
                    ]
                    peak = functools.reduce(jnp.maximum, [jnp.max(s, axis=0, keepdims=True) for s in logits])
                    own = [jnp.exp2(s - peak) for s in logits]
                    totals.append(functools.reduce(jnp.add, [jnp.sum(w, axis=0, keepdims=True) for w in own]))
                    weights.append([w.astype(BF16) for w in own])
                rows = pl.ds(64 * pair, 64)
                mixed = None
                for place in range(tiles):
                    v = v_ref[line, rows, k_at[place]]
                    zero = jnp.zeros_like(v)
                    spread = jnp.concatenate([jnp.where(upper, v, zero), jnp.where(upper, zero, v)], axis=1)
                    term = dot(spread, jnp.concatenate([weights[0][place], weights[1][place]], axis=0))
                    mixed = term if mixed is None else mixed + term
                inverse = [1.0 / total for total in totals]
                for sub in range(2):
                    at = pl.ds(64 * pair + 32 * sub, 32)
                    gated = mixed[32 * sub : 32 * sub + 32] * inverse[sub] * gate_ref[line, at, q_at]
                    mix_ref[line, at, q_at] = gated.astype(BF16)
            return carry

        lax.fori_loop(0, 8, body, 0)

    for tiles in range(1, 5):
        pl.when(count == tiles)(functools.partial(run, tiles))


def attention(which, mask, add, g, ids, steps, projected):
    return pl.pallas_call(
        functools.partial(attention_kernel, which),
        out_shape=jax.ShapeDtypeStruct((4, 128, 512), BF16),
        in_specs=[smem(), smem()] + [vmem()] * 7,
        out_specs=vmem(),
        scratch_shapes=[
            pltpu.VMEM((4, 4, 128, 512), F32),
            pltpu.VMEM((2048, 128), F32),
            pltpu.VMEM((4, 128, 128), F32),
        ],
        compiler_params=pltpu.CompilerParams(vmem_limit_bytes=VMEM_LIMIT),
        cost_estimate=cost(6),
        name=("row_attention", "col_attention")[which],
    )(mask, add, g, ids, steps, *projected)


def triangle_kernel(
    mask_ref,
    cols_ref,
    mix_ref,
    output_ref,
    left_ref,
    right_ref,
    gate_w_ref,
    out_w_ref,
    out_ref,
    cols_buf,
    edge_ref,
    second_ref,
    edge_in,
    second_in,
    edge_buf,
    prod_send,
    prod_in,
    x_buf,
    gate_buf,
    norm_buf,
    es,
    er,
    el,
    ss,
    sr,
    sl,
    ps,
    pr,
    pl_,
    second_round,
):
    row, col, dev = my_place()
    everyone = Everyone(second_round)
    flags = [mask_ref[tile, row // 4].astype(F32) for tile in range(4)]
    cols_buf[...] = cols_ref[...].astype(F32).reshape(2048, 128)
    w_o = output_ref[...]
    for line in range(4):
        value = cols_buf[pl.ds(line, 512, stride=4), :] + dot(mix_ref[line], w_o, 0, 0)
        rounded = value.astype(BF16)
        second_ref[:, line * 32 : (line + 1) * 32, :] = rounded.reshape(16, 32, 128)
        normed = layer_norm(rounded.astype(F32)).astype(BF16)
        for side, w_ref in enumerate((left_ref, right_ref)):
            both = dot(w_ref[...], normed, 0, 1)
            act = sigmoid(both[128:]) * both[:128]
            for tile in range(4):
                edge_buf[pl.ds(line * 8 + side * 4 + tile, 128, stride=32), :] = (
                    act[:, tile * 128 : (tile + 1) * 128] * flags[tile]
                )
        if line == 2:
            everyone.next_round()
    edge_ref[...] = edge_buf[...].reshape(128, 32, 128).astype(BF16)
    everyone.wait()
    edges = (edge_ref, edge_in, es, er, el)
    all_to_all_start(*edges)
    slot = lax.rem(dev, 16)
    grid_col = dev // 16

    def send_second(step, carry):
        to_row = lax.rem(row + step, 16)

        @pl.when(jnp.logical_and(to_row == row, grid_col == col))
        def _():
            pltpu.make_async_copy(second_ref.at[to_row], second_in.at[slot], sl).start()

        @pl.when(jnp.logical_not(jnp.logical_and(to_row == row, grid_col == col)))
        def _():
            pltpu.make_async_remote_copy(
                src_ref=second_ref.at[to_row],
                dst_ref=second_in.at[slot],
                send_sem=ss,
                recv_sem=sr,
                device_id=(to_row, grid_col),
                device_id_type=MESH,
            ).start()

        return carry

    all_to_all_recv(*edges)
    lax.fori_loop(0, 16, send_second, 0)
    edge_buf[...] = edge_in[...].astype(F32).reshape(4096, 128)
    right = jnp.concatenate([edge_buf[pl.ds(4 + tile, 512, stride=8), :] for tile in range(4)], axis=1).astype(BF16)
    low = lax.broadcasted_iota(jnp.int32, (16, 128), 1) < 64
    products = (prod_send, prod_in, ps, pr, pl_)

    def send_product(slab, first):
        def step(i, carry):
            dest = at_offset(slab * 32 + lax.rem(i * 13, 32))
            pltpu.make_async_remote_copy(
                src_ref=prod_send.at[dest],
                dst_ref=prod_in.at[dev],
                send_sem=ps,
                recv_sem=pr,
                device_id=(dest // 8, dest % 8),
                device_id_type=MESH,
            ).start()
            return carry

        lax.fori_loop(first, 32, step, 0)

    for slab in range(4):
        tile = lax.rem(row // 4 + slab, 4)
        left = edge_buf[pl.ds(tile, 512, stride=8), :].astype(BF16)
        product = dot(left, right, 0, 0)
        for sub in range(4):
            for t in range(4):
                a = product[sub * 32 : sub * 32 + 16, t * 128 : (t + 1) * 128]
                b = product[sub * 32 + 16 : sub * 32 + 32, t * 128 : (t + 1) * 128]
                block = tile * 32 + sub * 8 + 2 * t
                prod_send[block] = jnp.where(low, a, pltpu.roll(b, 64, 1)).astype(BF16)
                prod_send[block + 1] = jnp.where(low, pltpu.roll(a, 64, 1), b).astype(BF16)
        if slab == 0:
            pltpu.make_async_copy(prod_send.at[dev], prod_in.at[dev], pl_).start()
        send_product(slab, 1 if slab == 0 else 0)

    own_sent = grid_col == col

    @pl.when(own_sent)
    def _():
        drain(second_in.at[0], sl)
        drain(second_in.at[pl.ds(0, 15)], sr)
        drain(second_ref.at[pl.ds(0, 15)], ss)

    @pl.when(jnp.logical_not(own_sent))
    def _():
        drain(second_in, sr)
        drain(second_ref, ss)

    gate_w = gate_w_ref[...]

    def gates(j, carry):
        at = pl.multiple_of(j * 128, 128)
        x = second_in[j].astype(F32)
        gate = sigmoid(dot(layer_norm(x).astype(BF16), gate_w))
        for sub in range(4):
            x_buf[pl.ds(j * 4 + sub, 32, stride=64), :] = x[sub * 32 : (sub + 1) * 32]
            gate_buf[pl.ds(j * 4 + sub, 32, stride=64), :] = gate[sub * 32 : (sub + 1) * 32]
        return carry

    lax.fori_loop(0, 16, gates, 0)
    all_to_all_recv(*products)
    product = prod_in[...].astype(F32)
    center = product - jnp.mean(product, axis=0, keepdims=True)
    spread = jnp.mean(center * center, axis=0, keepdims=True)
    norm_buf[...] = (center * lax.rsqrt(spread + 1e-05)).reshape(2048, 128)
    out_w = out_w_ref[...]
    for s in range(16):
        update = dot(norm_buf[pl.ds(s, 128, stride=16), :].astype(BF16), out_w, 0, 0)
        for half in range(2):
            i = half * 16 + s
            at = pl.ds(i * 64, 64)
            out_ref[i] = (x_buf[at, :] + gate_buf[at, :] * update[half * 64 : (half + 1) * 64]).astype(BF16)
    all_to_all_sent(*edges)
    all_to_all_sent(*products)


def triangle(mask, cols, mix, output, left, right, gate_w, out_w):
    return pl.pallas_call(
        triangle_kernel,
        out_shape=jax.ShapeDtypeStruct((32, 64, 128), BF16),
        in_specs=[smem()] + [vmem()] * 7,
        out_specs=vmem(),
        scratch_shapes=[
            pltpu.VMEM((2048, 128), F32),
            pltpu.VMEM((128, 32, 128), BF16),
            pltpu.VMEM((16, 128, 128), BF16),
            pltpu.VMEM((128, 32, 128), BF16),
            pltpu.VMEM((16, 128, 128), BF16),
            pltpu.VMEM((4096, 128), F32),
            pltpu.VMEM((128, 16, 128), BF16),
            pltpu.VMEM((128, 16, 128), BF16),
            pltpu.VMEM((2048, 128), F32),
            pltpu.VMEM((2048, 128), F32),
            pltpu.VMEM((2048, 128), F32),
        ]
        + [pltpu.SemaphoreType.DMA] * 9
        + EVERYONE,
        compiler_params=pltpu.CompilerParams(
            collective_id=2, has_side_effects=True, vmem_limit_bytes=VMEM_LIMIT
        ),
        cost_estimate=cost(38),
        name="triangle",
    )(mask, cols, mix, output, left, right, gate_w, out_w)


def shards(
    pair_rep,
    tile_mask,
    chain_ids,
    chain_bias,
    row_project,
    row_bias_proj,
    row_output,
    col_project,
    col_bias_proj,
    col_output,
    tri_left,
    tri_right,
    tri_gate,
    tri_output,
):
    ids = chain_ids.reshape(1, 512)
    row_w, col_w = row_bias_proj.T, col_bias_proj.T
    mask, add = tile_mask, chain_bias
    g, *projected, steps = start(pair_rep, row_w, row_project)
    mix = attention(0, mask, add, g, ids, steps, projected)
    g, *projected, steps, cols = middle(pair_rep, mix, row_output, col_w, col_project)
    mix = attention(1, mask, add, g, ids, steps, projected)
    return triangle(mask, cols, mix, col_output, tri_left, tri_right, tri_gate, tri_output)


def solution(mesh):
    spec = P(("row", "col"), None, None)
    return jax.shard_map(
        shards,
        mesh=mesh,
        in_specs=(spec,) + (P(),) * 13,
        out_specs=P("row", "col", None),
        check_vma=False,
    )
```

```python
import functools
import math

import jax
import jax.numpy as jnp
from jax import lax
from jax.experimental import pallas as pl
from jax.experimental.pallas import tpu as pltpu
from jax.sharding import PartitionSpec as P

MESH = pl.DeviceIdType.MESH
F32 = jnp.float32
BF16 = jnp.bfloat16
DEVS = 128
LOG2E = 1.4426950408889634
VMEM_LIMIT = 24 * 2**20


def cost(microseconds):
    return pl.CostEstimate(flops=int(microseconds * 1.1e9), bytes_accessed=4 * 2**20, transcendentals=0)


def vmem():
    return pl.BlockSpec(memory_space=pltpu.VMEM)


def smem():
    return pl.BlockSpec(memory_space=pltpu.SMEM)


def layer_norm(values):
    center = values - jnp.mean(values, axis=-1, keepdims=True)
    spread = jnp.mean(center * center, axis=-1, keepdims=True)
    return center * lax.rsqrt(spread + 1e-05)


def dot(a, b, ca=1, cb=0):
    return lax.dot_general(a, b, (((ca,), (cb,)), ((), ())), preferred_element_type=F32)


def sigmoid(x):
    return 1.0 / (1.0 + jnp.exp(-x))


def my_place():
    row, col = lax.axis_index("row"), lax.axis_index("col")
    return row, col, row * 8 + col


def at_offset(offset):
    row, col, _ = my_place()
    x = lax.rem(row // 4 + offset // 32, 4)
    y = lax.rem(row % 4 + offset // 8 % 4, 4)
    z = lax.rem(col // 2 + offset // 2 % 4, 4)
    return ((x * 4 + y) * 4 + z) * 2 + lax.rem(col % 2 + offset % 2, 2)


def drain(ref, sem):
    pltpu.make_async_copy(ref, ref, sem).wait()


def bias_step(w_ref):
    w = w_ref[...].astype(F32)
    length = jnp.sqrt(jnp.sum(w * w, axis=1, keepdims=True))
    return jnp.maximum(length, 1e-20) * (11.4 / 32766.0)


def code_bias(blk32, line, w_ref, inverse, normed):
    coded = jnp.round(dot(w_ref[...], normed, 1, 1) * inverse).astype(jnp.int32)
    for tile in range(4):
        blk32[tile // 2, tile % 2, line * 4 : line * 4 + 4, :] = coded[:, tile * 128 : (tile + 1) * 128]


class Everyone:
    def __init__(self, second):
        self.second = second
        row, col, _ = my_place()
        x, y = row // 4, row % 4
        barrier = pltpu.get_barrier_semaphore()

        def step(i, carry):
            to = (x * 4 + lax.rem(y + i // 8, 4), lax.rem(col + i, 8))
            pl.semaphore_signal(barrier, inc=1, device_id=to, device_id_type=MESH)
            return carry

        lax.fori_loop(1, 32, step, 0)
        self.line = [(lax.rem(x + offset, 4) * 4 + y, col) for offset in (1, 2, 3)]
        for to in self.line:
            pl.semaphore_signal(barrier, inc=1, device_id=to, device_id_type=MESH)

    def next_round(self):
        await_signals(34)
        for to in self.line:
            pl.semaphore_signal(self.second, inc=1, device_id=to, device_id_type=MESH)

    def wait(self):
        pl.semaphore_wait(self.second, 3)


EVERYONE = [pltpu.SemaphoreType.REGULAR]


def await_signals(count):
    pl.semaphore_wait(pltpu.get_barrier_semaphore(), count)


G_SHAPE = (2, 128, 2, 16, 128)
GATHER_SEMS = [pltpu.SemaphoreType.DMA] * 3 + [pltpu.SemaphoreType.DMA((16,))] * 4


def near_row(half, offset):
    row, _, _ = my_place()
    y, x = row % 4, row // 4
    return jnp.where(half == 0, x * 4 + lax.rem(y + offset, 4), lax.rem(x + offset, 4) * 4 + y)


def far_row(half, offset):
    return near_row(1 - half, offset)


def signal_near():
    row, col, _ = my_place()
    core, z = col % 2, col // 2
    barrier = pltpu.get_barrier_semaphore()

    def step(i, carry):
        place = lax.rem(z + i // 2 % 4, 4) * 2 + lax.rem(core + i, 2)
        pl.semaphore_signal(barrier, inc=1, device_id=(near_row(core, i // 8), place), device_id_type=MESH)
        return carry

    lax.fori_loop(1, 32, step, 0)
    for offset in (1, 2, 3):
        pl.semaphore_signal(barrier, inc=1, device_id=(far_row(core, offset), col), device_id_type=MESH)
    return 34


def gather_bias(blk_ref, g_ref, own_sem, ns, nr, bs, br, fs, fr, work=()):
    row, col, dev = my_place()
    core, z, y, x = col % 2, col // 2, row % 4, row // 4
    sibling = (row, z * 2 + 1 - core)
    work = list(work)

    def do_work():
        if work:
            work.pop(0)()

    def part(half, start, size):
        return g_ref.at[half, pl.ds(start, size)]

    started = []

    def send(src, dst, ssem, rsem, device):
        copy = pltpu.make_async_remote_copy(
            src_ref=src, dst_ref=dst, send_sem=ssem, recv_sem=rsem, device_id=device, device_id_type=MESH
        )
        copy.start()
        started.append(copy)

    def send_near(half):
        def step(i, carry):
            to = lax.rem(i * 5, 16)
            pltpu.make_async_remote_copy(
                src_ref=blk_ref.at[pl.ds(half, 1)],
                dst_ref=g_ref.at[pl.ds(half, 1), dev],
                send_sem=ns,
                recv_sem=nr,
                device_id=(near_row(half, to // 4), lax.rem(z + to, 4) * 2 + half),
                device_id_type=MESH,
            ).start()
            return carry

        return step

    lax.fori_loop(1, 16, send_near(core), 0)
    lax.fori_loop(0, 16, send_near(1 - core), 0)
    own = pltpu.make_async_copy(blk_ref.at[pl.ds(core, 1)], g_ref.at[pl.ds(core, 1), dev], own_sem)
    own.start()
    do_work()
    own.wait()
    drain(g_ref.at[0, pl.ds(0, 31)], nr)

    def row_of(da, db):
        dx, dy = jnp.where(core == 0, db, da), jnp.where(core == 0, da, db)
        return lax.rem(x + dx, 4) * 4 + lax.rem(y + dy, 4)

    def block(da, db):
        return part(core, row_of(da, db) * 8, 8)

    def to_sibling(da, db):
        ref = block(da, db)
        send(ref, ref, fs.at[da * 4 + db], fr.at[da * 4 + db], sibling)

    for step in (1, 3, 2):
        for da in range(4):
            ref = block(da, 0)
            rel = 4 - step
            send(ref, ref, bs.at[da * 4 + rel], br.at[da * 4 + rel], (row_of(0, step), col))
    for da in range(4):
        to_sibling(da, 0)
    do_work()
    for db in (3, 1, 2):
        for da in range(4):
            drain(block(da, db), br.at[da * 4 + db])
            to_sibling(da, db)
    while work:
        do_work()
    for db in (0, 3, 1, 2):
        for da in range(4):
            drain(part(1 - core, row_of(db, da) * 8, 8), fr.at[da * 4 + db])
    for copy in started:
        copy.wait_send()
    drain(g_ref.at[0, pl.ds(0, 31)], ns)


PROJECTED = (
    jax.ShapeDtypeStruct((4, 512, 128), BF16),
    jax.ShapeDtypeStruct((4, 128, 512), BF16),
    jax.ShapeDtypeStruct((4, 128, 512), BF16),
    jax.ShapeDtypeStruct((4, 128, 512), F32),
)


def project_line(line, normed, project_ref, k_ref, q_ref, v_ref, gate_ref):
    k_ref[line] = dot(normed, project_ref[:, 128:256]).astype(BF16)
    q_ref[line] = dot(project_ref[:, 0:128], normed, 0, 1).astype(BF16)
    both = dot(project_ref[:, 256:512], normed, 0, 1)
    v_ref[line] = both[:128].astype(BF16)
    gate_ref[line] = sigmoid(both[128:])


BLK = [pltpu.VMEM((2, 2, 16, 128), jnp.int32), pltpu.VMEM((2, 2, 16, 128), jnp.int16)]
STEPS = jax.ShapeDtypeStruct((4, 128), F32)


def first_kernel(out_ref):
    out_ref[...] = jnp.zeros((8, 128), F32)


def first():
    return pl.pallas_call(
        first_kernel,
        out_shape=pltpu.VMEM((8, 128), F32),
        out_specs=vmem(),
        cost_estimate=cost(6),
        name="first",
    )()


def start_kernel(
    first_ref,
    x_ref,
    bias_w_ref,
    project_ref,
    g_ref,
    k_ref,
    q_ref,
    v_ref,
    gate_ref,
    steps_ref,
    blk32,
    blk,
    normed_buf,
    *sems,
):
    signals = signal_near()
    step = bias_step(bias_w_ref)
    steps_ref[...] = jnp.broadcast_to(step, (4, 128))
    inverse = 1.0 / step
    for line in range(4):
        normed = layer_norm(x_ref[line].astype(F32)).astype(BF16)
        normed_buf[line] = normed
        code_bias(blk32, line, bias_w_ref, inverse, normed)
    blk[...] = blk32[...].astype(jnp.int16)
    await_signals(signals)

    def work(lines):
        for line in lines:
            project_line(line, normed_buf[line], project_ref, k_ref, q_ref, v_ref, gate_ref)

    gather_bias(blk, g_ref, *sems, work=[functools.partial(work, lines) for lines in ((0, 1), (2, 3))])


def start(x, bias_w, project):
    return pl.pallas_call(
        start_kernel,
        out_shape=(jax.ShapeDtypeStruct(G_SHAPE, jnp.int16),) + PROJECTED + (STEPS,),
        in_specs=[vmem()] * 4,
        out_specs=(vmem(),) * 6,
        scratch_shapes=BLK + [pltpu.VMEM((4, 512, 128), BF16)] + GATHER_SEMS,
        compiler_params=pltpu.CompilerParams(
            collective_id=0, has_side_effects=True, vmem_limit_bytes=VMEM_LIMIT
        ),
        cost_estimate=cost(20),
        name="bias_gather",
    )(first(), x, bias_w, project)


def all_to_all_some(src_ref, dst_ref, ssem, rsem, lsem, first, last):
    row, col, dev = my_place()

    def step(i, carry):
        dest = at_offset(lax.rem(i * 37, DEVS))
        pltpu.make_async_remote_copy(
            src_ref=src_ref.at[dest],
            dst_ref=dst_ref.at[dev],
            send_sem=ssem,
            recv_sem=rsem,
            device_id=(dest // 8, dest % 8),
            device_id_type=MESH,
        ).start()
        return carry

    if first == 1:
        pltpu.make_async_copy(src_ref.at[dev], dst_ref.at[dev], lsem).start()
    lax.fori_loop(first, last, step, 0)


def all_to_all_start(*args):
    all_to_all_some(*args, 1, DEVS)


def all_to_all_recv(src_ref, dst_ref, ssem, rsem, lsem):
    drain(dst_ref.at[0], lsem)
    drain(dst_ref.at[pl.ds(0, DEVS - 1)], rsem)


def all_to_all_sent(src_ref, dst_ref, ssem, rsem, lsem):
    drain(src_ref.at[pl.ds(0, DEVS - 1)], ssem)


def middle_kernel(
    x_ref,
    mix_ref,
    output_ref,
    bias_w_ref,
    project_ref,
    g_ref,
    k_ref,
    q_ref,
    v_ref,
    gate_ref,
    steps_ref,
    cols_ref,
    line_buf,
    send_buf,
    tiles,
    cols_buf,
    blk32,
    blk,
    second_round,
    s0,
    s1,
    s2,
    *sems,
):
    everyone = Everyone(second_round)
    step = bias_step(bias_w_ref)
    steps_ref[...] = jnp.broadcast_to(step, (4, 128))
    inverse = 1.0 / step
    w_o = output_ref[...]
    for line in range(4):
        value = x_ref[line].astype(F32) + dot(mix_ref[line], w_o, 0, 0)
        value = value.astype(BF16).astype(F32)
        code_bias(blk32, line, bias_w_ref, inverse, layer_norm(value).astype(BF16))
        line_buf[line] = value
        for j in range(4):
            send_buf[pl.ds(line * 4 + j, 128, stride=16), :] = line_buf[line, pl.ds(j, 128, stride=4), :]
        if line == 2:
            everyone.next_round()
    blk[...] = blk32[...].astype(jnp.int16)
    tiles[...] = send_buf[...].reshape(128, 16, 128).astype(BF16)
    everyone.wait()
    args = (tiles, cols_ref, s0, s1, s2)

    def project_all():
        all_to_all_recv(*args)
        cols_buf[...] = cols_ref[...].astype(F32).reshape(2048, 128)
        for line in range(4):
            normed = layer_norm(cols_buf[pl.ds(line, 512, stride=4), :]).astype(BF16)
            project_line(line, normed, project_ref, k_ref, q_ref, v_ref, gate_ref)

    gather_bias(blk, g_ref, *sems, work=[functools.partial(all_to_all_start, *args), project_all])
    all_to_all_sent(*args)


def middle(x, mix, output, bias_w, project):
    return pl.pallas_call(
        middle_kernel,
        out_shape=(jax.ShapeDtypeStruct(G_SHAPE, jnp.int16),)
        + PROJECTED
        + (STEPS, jax.ShapeDtypeStruct((128, 16, 128), BF16)),
        in_specs=[vmem()] * 5,
        out_specs=(vmem(),) * 7,
        scratch_shapes=[
            pltpu.VMEM((4, 512, 128), F32),
            pltpu.VMEM((2048, 128), F32),
            pltpu.VMEM((128, 16, 128), BF16),
            pltpu.VMEM((2048, 128), F32),
        ]
        + BLK
        + EVERYONE
        + [pltpu.SemaphoreType.DMA] * 3
        + GATHER_SEMS,
        compiler_params=pltpu.CompilerParams(
            collective_id=1, has_side_effects=True, vmem_limit_bytes=VMEM_LIMIT
        ),
        cost_estimate=cost(28),
        name="columns_and_bias",
    )(x, mix, output, bias_w, project)


def compact(flags):
    count = jnp.int32(0)
    picked = [jnp.int32(0)] * 4
    for tile in range(4):
        for place in range(4):
            hit = jnp.logical_and(flags[tile] > 0, count == place)
            picked[place] = jnp.where(hit, tile, picked[place])
        count = count + flags[tile]
    return picked, count


def attention_kernel(
    which, mask_ref, add_ref, g_ref, ids_ref, steps_ref, k_ref, q_ref, v_ref, gate_ref, mix_ref, bias_buf, code_buf, ids_buf
):
    row, _, _ = my_place()
    flags = [mask_ref[row // 4, t] if which == 0 else mask_ref[t, row // 4] for t in range(4)]
    scale = LOG2E * 32 ** (-0.5)
    ids = ids_ref[...].astype(F32)
    for tile in range(4):
        ids_buf[tile] = jnp.broadcast_to(ids[:, tile * 128 : (tile + 1) * 128], (128, 128)).T
    picked, count = compact(flags)
    steps = steps_ref[...] * LOG2E
    adds = [add_ref[which, head] * LOG2E for head in range(4)]
    lanes = lax.broadcasted_iota(jnp.int32, (1, 128), 1) // 32
    head_masks = [jnp.where(lanes == head, 1.0, 0.0).astype(BF16) for head in range(4)]
    upper = lax.broadcasted_iota(jnp.int32, (64, 128), 0) < 32

    def run(tiles):
        def load_bias(place):
            tile = picked[place]
            if which == 0:
                code_buf[...] = g_ref[tile // 2, :, tile % 2].astype(F32).reshape(2048, 128)
            for q_tile in range(4):
                if which == 1:
                    got = g_ref[q_tile // 2, pl.ds(tile * 32, 32), q_tile % 2].astype(F32)
                    code_buf[0:512, :] = got.reshape(512, 128)
                same = ids_buf[tile] == ids[:, q_tile * 128 : (q_tile + 1) * 128]
                for head in range(4):
                    if which == 0:
                        code = code_buf[pl.ds(q_tile * 512 + head, 128, stride=4), :].T
                    else:
                        code = code_buf[pl.ds(head, 128, stride=4), :]
                    bias = code * steps[head : head + 1] + jnp.where(same, adds[head], 0.0)
                    bias_buf[head, place, :, q_tile * 128 : (q_tile + 1) * 128] = bias

        for place in range(tiles):
            load_bias(place)

        def body(step, carry):
            line, block = step // 2, step % 2
            q_at = pl.ds(pl.multiple_of(block * 256, 256), 256)
            q = q_ref[line, :, q_at]
            k_at = [pl.ds(pl.multiple_of(picked[place] * 128, 128), 128) for place in range(tiles)]
            scores = []
            for place in range(tiles):
                keys = k_ref[line, k_at[place], :]
                stacked = jnp.concatenate([keys * head_masks[head] for head in range(4)], axis=0)
                scores.append(dot(stacked, q))
            for pair in range(2):
                weights, totals = [], []
                for head in (2 * pair, 2 * pair + 1):
                    logits = [
                        scores[place][head * 128 : (head + 1) * 128] * scale + bias_buf[head, place, :, q_at]
                        for place in range(tiles)
                    ]
                    peak = functools.reduce(jnp.maximum, [jnp.max(s, axis=0, keepdims=True) for s in logits])
                    own = [jnp.exp2(s - peak) for s in logits]
                    totals.append(functools.reduce(jnp.add, [jnp.sum(w, axis=0, keepdims=True) for w in own]))
                    weights.append([w.astype(BF16) for w in own])
                rows = pl.ds(64 * pair, 64)
                mixed = None
                for place in range(tiles):
                    v = v_ref[line, rows, k_at[place]]
                    zero = jnp.zeros_like(v)
                    spread = jnp.concatenate([jnp.where(upper, v, zero), jnp.where(upper, zero, v)], axis=1)
                    term = dot(spread, jnp.concatenate([weights[0][place], weights[1][place]], axis=0))
                    mixed = term if mixed is None else mixed + term
                inverse = [1.0 / total for total in totals]
                for sub in range(2):
                    at = pl.ds(64 * pair + 32 * sub, 32)
                    gated = mixed[32 * sub : 32 * sub + 32] * inverse[sub] * gate_ref[line, at, q_at]
                    mix_ref[line, at, q_at] = gated.astype(BF16)
            return carry

        lax.fori_loop(0, 8, body, 0, unroll=(8, 4, 2, 2)[tiles - 1])

    for tiles in range(1, 5):
        pl.when(count == tiles)(functools.partial(run, tiles))


def attention(which, mask, add, g, ids, steps, projected):
    return pl.pallas_call(
        functools.partial(attention_kernel, which),
        out_shape=jax.ShapeDtypeStruct((4, 128, 512), BF16),
        in_specs=[smem(), smem()] + [vmem()] * 7,
        out_specs=vmem(),
        scratch_shapes=[
            pltpu.VMEM((4, 4, 128, 512), F32),
            pltpu.VMEM((2048, 128), F32),
            pltpu.VMEM((4, 128, 128), F32),
        ],
        compiler_params=pltpu.CompilerParams(vmem_limit_bytes=VMEM_LIMIT),
        cost_estimate=cost(6),
        name=("row_attention", "col_attention")[which],
    )(mask, add, g, ids, steps, *projected)


def triangle_kernel(
    mask_ref,
    cols_ref,
    mix_ref,
    output_ref,
    left_ref,
    right_ref,
    gate_w_ref,
    out_w_ref,
    out_ref,
    cols_buf,
    edge_ref,
    second_ref,
    edge_in,
    second_in,
    edge_buf,
    prod_send,
    prod_in,
    x_buf,
    gate_buf,
    norm_buf,
    es,
    er,
    el,
    ss,
    sr,
    sl,
    ps,
    pr,
    pl_,
    second_round,
):
    row, col, dev = my_place()
    everyone = Everyone(second_round)
    flags = [mask_ref[tile, row // 4].astype(F32) for tile in range(4)]
    cols_buf[...] = cols_ref[...].astype(F32).reshape(2048, 128)
    w_o = output_ref[...]
    for line in range(4):
        value = cols_buf[pl.ds(line, 512, stride=4), :] + dot(mix_ref[line], w_o, 0, 0)
        rounded = value.astype(BF16)
        second_ref[:, line * 32 : (line + 1) * 32, :] = rounded.reshape(16, 32, 128)
        normed = layer_norm(rounded.astype(F32)).astype(BF16)
        for side, w_ref in enumerate((left_ref, right_ref)):
            both = dot(w_ref[...], normed, 0, 1)
            act = sigmoid(both[128:]) * both[:128]
            for tile in range(4):
                edge_buf[pl.ds(line * 8 + side * 4 + tile, 128, stride=32), :] = (
                    act[:, tile * 128 : (tile + 1) * 128] * flags[tile]
                )
        if line == 2:
            everyone.next_round()
    edge_ref[...] = edge_buf[...].reshape(128, 32, 128).astype(BF16)
    everyone.wait()
    edges = (edge_ref, edge_in, es, er, el)
    all_to_all_start(*edges)
    slot = lax.rem(dev, 16)
    grid_col = dev // 16

    def send_second(step, carry):
        to_row = lax.rem(row + step, 16)

        @pl.when(jnp.logical_and(to_row == row, grid_col == col))
        def _():
            pltpu.make_async_copy(second_ref.at[to_row], second_in.at[slot], sl).start()

        @pl.when(jnp.logical_not(jnp.logical_and(to_row == row, grid_col == col)))
        def _():
            pltpu.make_async_remote_copy(
                src_ref=second_ref.at[to_row],
                dst_ref=second_in.at[slot],
                send_sem=ss,
                recv_sem=sr,
                device_id=(to_row, grid_col),
                device_id_type=MESH,
            ).start()

        return carry

    all_to_all_recv(*edges)
    lax.fori_loop(0, 16, send_second, 0)
    edge_buf[...] = edge_in[...].astype(F32).reshape(4096, 128)
    right = jnp.concatenate([edge_buf[pl.ds(4 + tile, 512, stride=8), :] for tile in range(4)], axis=1).astype(BF16)
    low = lax.broadcasted_iota(jnp.int32, (16, 128), 1) < 64
    products = (prod_send, prod_in, ps, pr, pl_)

    def send_product(slab, first):
        def step(i, carry):
            dest = at_offset(slab * 32 + lax.rem(i * 13, 32))
            pltpu.make_async_remote_copy(
                src_ref=prod_send.at[dest],
                dst_ref=prod_in.at[dev],
                send_sem=ps,
                recv_sem=pr,
                device_id=(dest // 8, dest % 8),
                device_id_type=MESH,
            ).start()
            return carry

        lax.fori_loop(first, 32, step, 0)

    for slab in range(4):
        tile = lax.rem(row // 4 + slab, 4)
        left = edge_buf[pl.ds(tile, 512, stride=8), :].astype(BF16)
        product = dot(left, right, 0, 0)
        for sub in range(4):
            for t in range(4):
                a = product[sub * 32 : sub * 32 + 16, t * 128 : (t + 1) * 128]
                b = product[sub * 32 + 16 : sub * 32 + 32, t * 128 : (t + 1) * 128]
                block = tile * 32 + sub * 8 + 2 * t
                prod_send[block] = jnp.where(low, a, pltpu.roll(b, 64, 1)).astype(BF16)
                prod_send[block + 1] = jnp.where(low, pltpu.roll(a, 64, 1), b).astype(BF16)
        if slab == 0:
            pltpu.make_async_copy(prod_send.at[dev], prod_in.at[dev], pl_).start()
        send_product(slab, 1 if slab == 0 else 0)

    own_sent = grid_col == col

    @pl.when(own_sent)
    def _():
        drain(second_in.at[0], sl)
        drain(second_in.at[pl.ds(0, 15)], sr)
        drain(second_ref.at[pl.ds(0, 15)], ss)

    @pl.when(jnp.logical_not(own_sent))
    def _():
        drain(second_in, sr)
        drain(second_ref, ss)

    gate_w = gate_w_ref[...]

    def gates(j, carry):
        at = pl.multiple_of(j * 128, 128)
        x = second_in[j].astype(F32)
        gate = sigmoid(dot(layer_norm(x).astype(BF16), gate_w))
        for sub in range(4):
            x_buf[pl.ds(j * 4 + sub, 32, stride=64), :] = x[sub * 32 : (sub + 1) * 32]
            gate_buf[pl.ds(j * 4 + sub, 32, stride=64), :] = gate[sub * 32 : (sub + 1) * 32]
        return carry

    lax.fori_loop(0, 16, gates, 0)
    all_to_all_recv(*products)
    product = prod_in[...].astype(F32)
    center = product - jnp.mean(product, axis=0, keepdims=True)
    spread = jnp.mean(center * center, axis=0, keepdims=True)
    norm_buf[...] = (center * lax.rsqrt(spread + 1e-05)).reshape(2048, 128)
    out_w = out_w_ref[...]
    for s in range(16):
        update = dot(norm_buf[pl.ds(s, 128, stride=16), :].astype(BF16), out_w, 0, 0)
        for half in range(2):
            i = half * 16 + s
            at = pl.ds(i * 64, 64)
            out_ref[i] = (x_buf[at, :] + gate_buf[at, :] * update[half * 64 : (half + 1) * 64]).astype(BF16)
    all_to_all_sent(*edges)
    all_to_all_sent(*products)


def triangle(mask, cols, mix, output, left, right, gate_w, out_w):
    return pl.pallas_call(
        triangle_kernel,
        out_shape=jax.ShapeDtypeStruct((32, 64, 128), BF16),
        in_specs=[smem()] + [vmem()] * 7,
        out_specs=vmem(),
        scratch_shapes=[
            pltpu.VMEM((2048, 128), F32),
            pltpu.VMEM((128, 32, 128), BF16),
            pltpu.VMEM((16, 128, 128), BF16),
            pltpu.VMEM((128, 32, 128), BF16),
            pltpu.VMEM((16, 128, 128), BF16),
            pltpu.VMEM((4096, 128), F32),
            pltpu.VMEM((128, 16, 128), BF16),
            pltpu.VMEM((128, 16, 128), BF16),
            pltpu.VMEM((2048, 128), F32),
            pltpu.VMEM((2048, 128), F32),
            pltpu.VMEM((2048, 128), F32),
        ]
        + [pltpu.SemaphoreType.DMA] * 9
        + EVERYONE,
        compiler_params=pltpu.CompilerParams(
            collective_id=2, has_side_effects=True, vmem_limit_bytes=VMEM_LIMIT
        ),
        cost_estimate=cost(38),
        name="triangle",
    )(mask, cols, mix, output, left, right, gate_w, out_w)


def shards(
    pair_rep,
    tile_mask,
    chain_ids,
    chain_bias,
    row_project,
    row_bias_proj,
    row_output,
    col_project,
    col_bias_proj,
    col_output,
    tri_left,
    tri_right,
    tri_gate,
    tri_output,
):
    ids = chain_ids.reshape(1, 512)
    row_w, col_w = row_bias_proj.T, col_bias_proj.T
    mask, add = tile_mask, chain_bias
    g, *projected, steps = start(pair_rep, row_w, row_project)
    mix = attention(0, mask, add, g, ids, steps, projected)
    g, *projected, steps, cols = middle(pair_rep, mix, row_output, col_w, col_project)
    mix = attention(1, mask, add, g, ids, steps, projected)
    return triangle(mask, cols, mix, col_output, tri_left, tri_right, tri_gate, tri_output)


def solution(mesh):
    spec = P(("row", "col"), None, None)
    return jax.shard_map(
        shards,
        mesh=mesh,
        in_specs=(spec,) + (P(),) * 13,
        out_specs=P("row", "col", None),
        check_vma=False,
    )
```

```python
import functools
import math

import jax
import jax.numpy as jnp
from jax import lax
from jax.experimental import pallas as pl
from jax.experimental.pallas import tpu as pltpu
from jax.sharding import PartitionSpec as P

MESH = pl.DeviceIdType.MESH
F32 = jnp.float32
BF16 = jnp.bfloat16
DEVS = 128
LOG2E = 1.4426950408889634
VMEM_LIMIT = 24 * 2**20


def cost(microseconds):
    return pl.CostEstimate(flops=int(microseconds * 1.1e9), bytes_accessed=4 * 2**20, transcendentals=0)


def vmem():
    return pl.BlockSpec(memory_space=pltpu.VMEM)


def smem():
    return pl.BlockSpec(memory_space=pltpu.SMEM)


def layer_norm(values):
    center = values - jnp.mean(values, axis=-1, keepdims=True)
    spread = jnp.mean(center * center, axis=-1, keepdims=True)
    return center * lax.rsqrt(spread + 1e-05)


def dot(a, b, ca=1, cb=0):
    return lax.dot_general(a, b, (((ca,), (cb,)), ((), ())), preferred_element_type=F32)


def sigmoid(x):
    return 1.0 / (1.0 + jnp.exp(-x))


def my_place():
    row, col = lax.axis_index("row"), lax.axis_index("col")
    return row, col, row * 8 + col


def at_offset(offset):
    row, col, _ = my_place()
    x = lax.rem(row // 4 + offset // 32, 4)
    y = lax.rem(row % 4 + offset // 8 % 4, 4)
    z = lax.rem(col // 2 + offset // 2 % 4, 4)
    return ((x * 4 + y) * 4 + z) * 2 + lax.rem(col % 2 + offset % 2, 2)


def drain(ref, sem):
    pltpu.make_async_copy(ref, ref, sem).wait()


def bias_step(w_ref):
    w = w_ref[...].astype(F32)
    length = jnp.sqrt(jnp.sum(w * w, axis=1, keepdims=True))
    return jnp.maximum(length, 1e-20) * (11.4 / 32766.0)


def code_bias(blk32, line, w_ref, inverse, normed):
    coded = jnp.round(dot(w_ref[...], normed, 1, 1) * inverse).astype(jnp.int32)
    for tile in range(4):
        blk32[tile // 2, tile % 2, line * 4 : line * 4 + 4, :] = coded[:, tile * 128 : (tile + 1) * 128]


class Everyone:
    def __init__(self, second):
        self.second = second
        row, col, _ = my_place()
        x, y = row // 4, row % 4
        barrier = pltpu.get_barrier_semaphore()

        def step(i, carry):
            to = (x * 4 + lax.rem(y + i // 8, 4), lax.rem(col + i, 8))
            pl.semaphore_signal(barrier, inc=1, device_id=to, device_id_type=MESH)
            return carry

        lax.fori_loop(1, 32, step, 0)
        self.line = [(lax.rem(x + offset, 4) * 4 + y, col) for offset in (1, 2, 3)]
        for to in self.line:
            pl.semaphore_signal(barrier, inc=1, device_id=to, device_id_type=MESH)

    def next_round(self):
        await_signals(34)
        for to in self.line:
            pl.semaphore_signal(self.second, inc=1, device_id=to, device_id_type=MESH)

    def wait(self):
        pl.semaphore_wait(self.second, 3)


EVERYONE = [pltpu.SemaphoreType.REGULAR]


def await_signals(count):
    pl.semaphore_wait(pltpu.get_barrier_semaphore(), count)


G_SHAPE = (2, 128, 2, 16, 128)
GATHER_SEMS = [pltpu.SemaphoreType.DMA] * 3 + [pltpu.SemaphoreType.DMA((16,))] * 4


def near_row(half, offset):
    row, _, _ = my_place()
    y, x = row % 4, row // 4
    return jnp.where(half == 0, x * 4 + lax.rem(y + offset, 4), lax.rem(x + offset, 4) * 4 + y)


def far_row(half, offset):
    return near_row(1 - half, offset)


def signal_near():
    row, col, _ = my_place()
    core, z = col % 2, col // 2
    barrier = pltpu.get_barrier_semaphore()

    def step(i, carry):
        place = lax.rem(z + i // 2 % 4, 4) * 2 + lax.rem(core + i, 2)
        pl.semaphore_signal(barrier, inc=1, device_id=(near_row(core, i // 8), place), device_id_type=MESH)
        return carry

    lax.fori_loop(1, 32, step, 0)
    for offset in (1, 2, 3):
        pl.semaphore_signal(barrier, inc=1, device_id=(far_row(core, offset), col), device_id_type=MESH)
    return 34


def gather_bias(blk_ref, g_ref, own_sem, ns, nr, bs, br, fs, fr, work=()):
    row, col, dev = my_place()
    core, z, y, x = col % 2, col // 2, row % 4, row // 4
    sibling = (row, z * 2 + 1 - core)
    work = list(work)

    def do_work():
        if work:
            work.pop(0)()

    def part(half, start, size):
        return g_ref.at[half, pl.ds(start, size)]

    started = []

    def send(src, dst, ssem, rsem, device):
        copy = pltpu.make_async_remote_copy(
            src_ref=src, dst_ref=dst, send_sem=ssem, recv_sem=rsem, device_id=device, device_id_type=MESH
        )
        copy.start()
        started.append(copy)

    def send_near(half):
        def step(i, carry):
            to = lax.rem(i * 5, 16)
            pltpu.make_async_remote_copy(
                src_ref=blk_ref.at[pl.ds(half, 1)],
                dst_ref=g_ref.at[pl.ds(half, 1), dev],
                send_sem=ns,
                recv_sem=nr,
                device_id=(near_row(half, to // 4), lax.rem(z + to, 4) * 2 + half),
                device_id_type=MESH,
            ).start()
            return carry

        return step

    lax.fori_loop(1, 16, send_near(core), 0)
    lax.fori_loop(0, 16, send_near(1 - core), 0)
    own = pltpu.make_async_copy(blk_ref.at[pl.ds(core, 1)], g_ref.at[pl.ds(core, 1), dev], own_sem)
    own.start()
    do_work()
    own.wait()
    drain(g_ref.at[0, pl.ds(0, 31)], nr)

    def row_of(da, db):
        dx, dy = jnp.where(core == 0, db, da), jnp.where(core == 0, da, db)
        return lax.rem(x + dx, 4) * 4 + lax.rem(y + dy, 4)

    def block(da, db):
        return part(core, row_of(da, db) * 8, 8)

    def to_sibling(da, db):
        ref = block(da, db)
        send(ref, ref, fs.at[da * 4 + db], fr.at[da * 4 + db], sibling)

    for step in (1, 3, 2):
        for da in range(4):
            ref = block(da, 0)
            rel = 4 - step
            send(ref, ref, bs.at[da * 4 + rel], br.at[da * 4 + rel], (row_of(0, step), col))
    for da in range(4):
        to_sibling(da, 0)
    do_work()
    for db in (3, 1, 2):
        for da in range(4):
            drain(block(da, db), br.at[da * 4 + db])
            to_sibling(da, db)
    while work:
        do_work()
    for db in (0, 3, 1, 2):
        for da in range(4):
            drain(part(1 - core, row_of(db, da) * 8, 8), fr.at[da * 4 + db])
    for copy in started:
        copy.wait_send()
    drain(g_ref.at[0, pl.ds(0, 31)], ns)


PROJECTED = (
    jax.ShapeDtypeStruct((4, 512, 128), BF16),
    jax.ShapeDtypeStruct((4, 128, 512), BF16),
    jax.ShapeDtypeStruct((4, 128, 512), BF16),
    jax.ShapeDtypeStruct((4, 128, 512), F32),
)


def project_line(line, normed, project_ref, k_ref, q_ref, v_ref, gate_ref):
    k_ref[line] = dot(normed, project_ref[:, 128:256]).astype(BF16)
    q_ref[line] = dot(project_ref[:, 0:128], normed, 0, 1).astype(BF16)
    both = dot(project_ref[:, 256:512], normed, 0, 1)
    v_ref[line] = both[:128].astype(BF16)
    gate_ref[line] = sigmoid(both[128:])


BLK = [pltpu.VMEM((2, 2, 16, 128), jnp.int32), pltpu.VMEM((2, 2, 16, 128), jnp.int16)]
STEPS = jax.ShapeDtypeStruct((4, 128), F32)


def first_kernel(out_ref):
    out_ref[...] = jnp.zeros((8, 128), F32)


def first():
    return pl.pallas_call(
        first_kernel,
        out_shape=pltpu.VMEM((8, 128), F32),
        out_specs=vmem(),
        cost_estimate=cost(6),
        name="first",
    )()


def start_kernel(
    first_ref,
    x_ref,
    bias_w_ref,
    project_ref,
    g_ref,
    k_ref,
    q_ref,
    v_ref,
    gate_ref,
    steps_ref,
    blk32,
    blk,
    normed_buf,
    *sems,
):
    signals = signal_near()
    step = bias_step(bias_w_ref)
    steps_ref[...] = jnp.broadcast_to(step, (4, 128))
    inverse = 1.0 / step
    for line in range(4):
        normed = layer_norm(x_ref[line].astype(F32)).astype(BF16)
        normed_buf[line] = normed
        code_bias(blk32, line, bias_w_ref, inverse, normed)
    blk[...] = blk32[...].astype(jnp.int16)
    await_signals(signals)

    def work(lines):
        for line in lines:
            project_line(line, normed_buf[line], project_ref, k_ref, q_ref, v_ref, gate_ref)

    gather_bias(blk, g_ref, *sems, work=[functools.partial(work, lines) for lines in ((0, 1), (2, 3))])


def start(x, bias_w, project):
    return pl.pallas_call(
        start_kernel,
        out_shape=(jax.ShapeDtypeStruct(G_SHAPE, jnp.int16),) + PROJECTED + (STEPS,),
        in_specs=[vmem()] * 4,
        out_specs=(vmem(),) * 6,
        scratch_shapes=BLK + [pltpu.VMEM((4, 512, 128), BF16)] + GATHER_SEMS,
        compiler_params=pltpu.CompilerParams(
            collective_id=0, has_side_effects=True, vmem_limit_bytes=VMEM_LIMIT
        ),
        cost_estimate=cost(20),
        name="bias_gather",
    )(first(), x, bias_w, project)


def all_to_all_some(src_ref, dst_ref, ssem, rsem, lsem, first, last):
    row, col, dev = my_place()

    def step(i, carry):
        dest = at_offset(lax.rem(i * 37, DEVS))
        pltpu.make_async_remote_copy(
            src_ref=src_ref.at[dest],
            dst_ref=dst_ref.at[dev],
            send_sem=ssem,
            recv_sem=rsem,
            device_id=(dest // 8, dest % 8),
            device_id_type=MESH,
        ).start()
        return carry

    if first == 1:
        pltpu.make_async_copy(src_ref.at[dev], dst_ref.at[dev], lsem).start()
    lax.fori_loop(first, last, step, 0)


def all_to_all_start(*args):
    all_to_all_some(*args, 1, DEVS)


def all_to_all_recv(src_ref, dst_ref, ssem, rsem, lsem):
    drain(dst_ref.at[0], lsem)
    drain(dst_ref.at[pl.ds(0, DEVS - 1)], rsem)


def all_to_all_sent(src_ref, dst_ref, ssem, rsem, lsem):
    drain(src_ref.at[pl.ds(0, DEVS - 1)], ssem)


def middle_kernel(
    x_ref,
    mix_ref,
    output_ref,
    bias_w_ref,
    project_ref,
    g_ref,
    k_ref,
    q_ref,
    v_ref,
    gate_ref,
    steps_ref,
    cols_ref,
    line_buf,
    send_buf,
    tiles,
    cols_buf,
    blk32,
    blk,
    second_round,
    s0,
    s1,
    s2,
    *sems,
):
    everyone = Everyone(second_round)
    step = bias_step(bias_w_ref)
    steps_ref[...] = jnp.broadcast_to(step, (4, 128))
    inverse = 1.0 / step
    w_o = output_ref[...]
    for line in range(4):
        value = x_ref[line].astype(F32) + dot(mix_ref[line], w_o, 0, 0)
        value = value.astype(BF16).astype(F32)
        code_bias(blk32, line, bias_w_ref, inverse, layer_norm(value).astype(BF16))
        line_buf[line] = value
        for j in range(4):
            send_buf[pl.ds(line * 4 + j, 128, stride=16), :] = line_buf[line, pl.ds(j, 128, stride=4), :]
        if line == 3:
            everyone.next_round()
    blk[...] = blk32[...].astype(jnp.int16)
    tiles[...] = send_buf[...].reshape(128, 16, 128).astype(BF16)
    everyone.wait()
    args = (tiles, cols_ref, s0, s1, s2)

    def project_all():
        all_to_all_recv(*args)
        cols_buf[...] = cols_ref[...].astype(F32).reshape(2048, 128)
        for line in range(4):
            normed = layer_norm(cols_buf[pl.ds(line, 512, stride=4), :]).astype(BF16)
            project_line(line, normed, project_ref, k_ref, q_ref, v_ref, gate_ref)

    gather_bias(blk, g_ref, *sems, work=[functools.partial(all_to_all_start, *args), project_all])
    all_to_all_sent(*args)


def middle(x, mix, output, bias_w, project):
    return pl.pallas_call(
        middle_kernel,
        out_shape=(jax.ShapeDtypeStruct(G_SHAPE, jnp.int16),)
        + PROJECTED
        + (STEPS, jax.ShapeDtypeStruct((128, 16, 128), BF16)),
        in_specs=[vmem()] * 5,
        out_specs=(vmem(),) * 7,
        scratch_shapes=[
            pltpu.VMEM((4, 512, 128), F32),
            pltpu.VMEM((2048, 128), F32),
            pltpu.VMEM((128, 16, 128), BF16),
            pltpu.VMEM((2048, 128), F32),
        ]
        + BLK
        + EVERYONE
        + [pltpu.SemaphoreType.DMA] * 3
        + GATHER_SEMS,
        compiler_params=pltpu.CompilerParams(
            collective_id=1, has_side_effects=True, vmem_limit_bytes=VMEM_LIMIT
        ),
        cost_estimate=cost(28),
        name="columns_and_bias",
    )(x, mix, output, bias_w, project)


def compact(flags):
    count = jnp.int32(0)
    picked = [jnp.int32(0)] * 4
    for tile in range(4):
        for place in range(4):
            hit = jnp.logical_and(flags[tile] > 0, count == place)
            picked[place] = jnp.where(hit, tile, picked[place])
        count = count + flags[tile]
    return picked, count


def attention_kernel(
    which, mask_ref, add_ref, g_ref, ids_ref, steps_ref, k_ref, q_ref, v_ref, gate_ref, mix_ref, bias_buf, code_buf, ids_buf
):
    row, _, _ = my_place()
    flags = [mask_ref[row // 4, t] if which == 0 else mask_ref[t, row // 4] for t in range(4)]
    scale = LOG2E * 32 ** (-0.5)
    ids = ids_ref[...].astype(F32)
    for tile in range(4):
        ids_buf[tile] = jnp.broadcast_to(ids[:, tile * 128 : (tile + 1) * 128], (128, 128)).T
    picked, count = compact(flags)
    steps = steps_ref[...] * LOG2E
    adds = [add_ref[which, head] * LOG2E for head in range(4)]
    lanes = lax.broadcasted_iota(jnp.int32, (1, 128), 1) // 32
    head_masks = [jnp.where(lanes == head, 1.0, 0.0).astype(BF16) for head in range(4)]
    upper = lax.broadcasted_iota(jnp.int32, (64, 128), 0) < 32

    def run(tiles):
        def load_bias(place):
            tile = picked[place]
            if which == 0:
                code_buf[...] = g_ref[tile // 2, :, tile % 2].astype(F32).reshape(2048, 128)
            for q_tile in range(4):
                if which == 1:
                    got = g_ref[q_tile // 2, pl.ds(tile * 32, 32), q_tile % 2].astype(F32)
                    code_buf[0:512, :] = got.reshape(512, 128)
                same = ids_buf[tile] == ids[:, q_tile * 128 : (q_tile + 1) * 128]
                for head in range(4):
                    if which == 0:
                        code = code_buf[pl.ds(q_tile * 512 + head, 128, stride=4), :].T
                    else:
                        code = code_buf[pl.ds(head, 128, stride=4), :]
                    bias = code * steps[head : head + 1] + jnp.where(same, adds[head], 0.0)
                    bias_buf[head, place, :, q_tile * 128 : (q_tile + 1) * 128] = bias

        for place in range(tiles):
            load_bias(place)

        def body(step, carry):
            line, block = step // 2, step % 2
            q_at = pl.ds(pl.multiple_of(block * 256, 256), 256)
            q = q_ref[line, :, q_at]
            k_at = [pl.ds(pl.multiple_of(picked[place] * 128, 128), 128) for place in range(tiles)]
            scores = []
            for place in range(tiles):
                keys = k_ref[line, k_at[place], :]
                stacked = jnp.concatenate([keys * head_masks[head] for head in range(4)], axis=0)
                scores.append(dot(stacked, q))
            for pair in range(2):
                weights, totals = [], []
                for head in (2 * pair, 2 * pair + 1):
                    logits = [
                        scores[place][head * 128 : (head + 1) * 128] * scale + bias_buf[head, place, :, q_at]
                        for place in range(tiles)
                    ]
                    peak = functools.reduce(jnp.maximum, [jnp.max(s, axis=0, keepdims=True) for s in logits])
                    own = [jnp.exp2(s - peak) for s in logits]
                    totals.append(functools.reduce(jnp.add, [jnp.sum(w, axis=0, keepdims=True) for w in own]))
                    weights.append([w.astype(BF16) for w in own])
                rows = pl.ds(64 * pair, 64)
                mixed = None
                for place in range(tiles):
                    v = v_ref[line, rows, k_at[place]]
                    zero = jnp.zeros_like(v)
                    spread = jnp.concatenate([jnp.where(upper, v, zero), jnp.where(upper, zero, v)], axis=1)
                    term = dot(spread, jnp.concatenate([weights[0][place], weights[1][place]], axis=0))
                    mixed = term if mixed is None else mixed + term
                inverse = [1.0 / total for total in totals]
                for sub in range(2):
                    at = pl.ds(64 * pair + 32 * sub, 32)
                    gated = mixed[32 * sub : 32 * sub + 32] * inverse[sub] * gate_ref[line, at, q_at]
                    mix_ref[line, at, q_at] = gated.astype(BF16)
            return carry

        lax.fori_loop(0, 8, body, 0, unroll=(8, 4, 2, 2)[tiles - 1])

    for tiles in range(1, 5):
        pl.when(count == tiles)(functools.partial(run, tiles))


def attention(which, mask, add, g, ids, steps, projected):
    return pl.pallas_call(
        functools.partial(attention_kernel, which),
        out_shape=jax.ShapeDtypeStruct((4, 128, 512), BF16),
        in_specs=[smem(), smem()] + [vmem()] * 7,
        out_specs=vmem(),
        scratch_shapes=[
            pltpu.VMEM((4, 4, 128, 512), F32),
            pltpu.VMEM((2048, 128), F32),
            pltpu.VMEM((4, 128, 128), F32),
        ],
        compiler_params=pltpu.CompilerParams(vmem_limit_bytes=VMEM_LIMIT),
        cost_estimate=cost(6),
        name=("row_attention", "col_attention")[which],
    )(mask, add, g, ids, steps, *projected)


def triangle_kernel(
    mask_ref,
    cols_ref,
    mix_ref,
    output_ref,
    left_ref,
    right_ref,
    gate_w_ref,
    out_w_ref,
    out_ref,
    cols_buf,
    edge_ref,
    second_ref,
    edge_in,
    second_in,
    edge_buf,
    prod_send,
    prod_in,
    x_buf,
    gate_buf,
    norm_buf,
    es,
    er,
    el,
    ss,
    sr,
    sl,
    ps,
    pr,
    pl_,
    second_round,
):
    row, col, dev = my_place()
    everyone = Everyone(second_round)
    flags = [mask_ref[tile, row // 4].astype(F32) for tile in range(4)]
    cols_buf[...] = cols_ref[...].astype(F32).reshape(2048, 128)
    w_o = output_ref[...]
    for line in range(4):
        value = cols_buf[pl.ds(line, 512, stride=4), :] + dot(mix_ref[line], w_o, 0, 0)
        rounded = value.astype(BF16)
        second_ref[:, line * 32 : (line + 1) * 32, :] = rounded.reshape(16, 32, 128)
        normed = layer_norm(rounded.astype(F32)).astype(BF16)
        for side, w_ref in enumerate((left_ref, right_ref)):
            both = dot(w_ref[...], normed, 0, 1)
            act = sigmoid(both[128:]) * both[:128]
            for tile in range(4):
                edge_buf[pl.ds(line * 8 + side * 4 + tile, 128, stride=32), :] = (
                    act[:, tile * 128 : (tile + 1) * 128] * flags[tile]
                )
        if line == 3:
            everyone.next_round()
    edge_ref[...] = edge_buf[...].reshape(128, 32, 128).astype(BF16)
    everyone.wait()
    edges = (edge_ref, edge_in, es, er, el)
    all_to_all_start(*edges)
    slot = lax.rem(dev, 16)
    grid_col = dev // 16

    def send_second(step, carry):
        to_row = lax.rem(row + step, 16)

        @pl.when(jnp.logical_and(to_row == row, grid_col == col))
        def _():
            pltpu.make_async_copy(second_ref.at[to_row], second_in.at[slot], sl).start()

        @pl.when(jnp.logical_not(jnp.logical_and(to_row == row, grid_col == col)))
        def _():
            pltpu.make_async_remote_copy(
                src_ref=second_ref.at[to_row],
                dst_ref=second_in.at[slot],
                send_sem=ss,
                recv_sem=sr,
                device_id=(to_row, grid_col),
                device_id_type=MESH,
            ).start()

        return carry

    all_to_all_recv(*edges)
    lax.fori_loop(0, 16, send_second, 0)
    edge_buf[...] = edge_in[...].astype(F32).reshape(4096, 128)
    right = jnp.concatenate([edge_buf[pl.ds(4 + tile, 512, stride=8), :] for tile in range(4)], axis=1).astype(BF16)
    low = lax.broadcasted_iota(jnp.int32, (16, 128), 1) < 64
    products = (prod_send, prod_in, ps, pr, pl_)

    def send_product(slab, first):
        def step(i, carry):
            dest = at_offset(slab * 32 + lax.rem(i * 13, 32))
            pltpu.make_async_remote_copy(
                src_ref=prod_send.at[dest],
                dst_ref=prod_in.at[dev],
                send_sem=ps,
                recv_sem=pr,
                device_id=(dest // 8, dest % 8),
                device_id_type=MESH,
            ).start()
            return carry

        lax.fori_loop(first, 32, step, 0)

    for slab in range(4):
        tile = lax.rem(row // 4 + slab, 4)
        left = edge_buf[pl.ds(tile, 512, stride=8), :].astype(BF16)
        product = dot(left, right, 0, 0)
        for sub in range(4):
            for t in range(4):
                a = product[sub * 32 : sub * 32 + 16, t * 128 : (t + 1) * 128]
                b = product[sub * 32 + 16 : sub * 32 + 32, t * 128 : (t + 1) * 128]
                block = tile * 32 + sub * 8 + 2 * t
                prod_send[block] = jnp.where(low, a, pltpu.roll(b, 64, 1)).astype(BF16)
                prod_send[block + 1] = jnp.where(low, pltpu.roll(a, 64, 1), b).astype(BF16)
        if slab == 0:
            pltpu.make_async_copy(prod_send.at[dev], prod_in.at[dev], pl_).start()
        send_product(slab, 1 if slab == 0 else 0)

    own_sent = grid_col == col

    @pl.when(own_sent)
    def _():
        drain(second_in.at[0], sl)
        drain(second_in.at[pl.ds(0, 15)], sr)
        drain(second_ref.at[pl.ds(0, 15)], ss)

    @pl.when(jnp.logical_not(own_sent))
    def _():
        drain(second_in, sr)
        drain(second_ref, ss)

    gate_w = gate_w_ref[...]

    def gates(j, carry):
        at = pl.multiple_of(j * 128, 128)
        x = second_in[j].astype(F32)
        gate = sigmoid(dot(layer_norm(x).astype(BF16), gate_w))
        for sub in range(4):
            x_buf[pl.ds(j * 4 + sub, 32, stride=64), :] = x[sub * 32 : (sub + 1) * 32]
            gate_buf[pl.ds(j * 4 + sub, 32, stride=64), :] = gate[sub * 32 : (sub + 1) * 32]
        return carry

    lax.fori_loop(0, 16, gates, 0)
    all_to_all_recv(*products)
    product = prod_in[...].astype(F32)
    center = product - jnp.mean(product, axis=0, keepdims=True)
    spread = jnp.mean(center * center, axis=0, keepdims=True)
    norm_buf[...] = (center * lax.rsqrt(spread + 1e-05)).reshape(2048, 128)
    out_w = out_w_ref[...]
    for s in range(16):
        update = dot(norm_buf[pl.ds(s, 128, stride=16), :].astype(BF16), out_w, 0, 0)
        for half in range(2):
            i = half * 16 + s
            at = pl.ds(i * 64, 64)
            out_ref[i] = (x_buf[at, :] + gate_buf[at, :] * update[half * 64 : (half + 1) * 64]).astype(BF16)
    all_to_all_sent(*edges)
    all_to_all_sent(*products)


def triangle(mask, cols, mix, output, left, right, gate_w, out_w):
    return pl.pallas_call(
        triangle_kernel,
        out_shape=jax.ShapeDtypeStruct((32, 64, 128), BF16),
        in_specs=[smem()] + [vmem()] * 7,
        out_specs=vmem(),
        scratch_shapes=[
            pltpu.VMEM((2048, 128), F32),
            pltpu.VMEM((128, 32, 128), BF16),
            pltpu.VMEM((16, 128, 128), BF16),
            pltpu.VMEM((128, 32, 128), BF16),
            pltpu.VMEM((16, 128, 128), BF16),
            pltpu.VMEM((4096, 128), F32),
            pltpu.VMEM((128, 16, 128), BF16),
            pltpu.VMEM((128, 16, 128), BF16),
            pltpu.VMEM((2048, 128), F32),
            pltpu.VMEM((2048, 128), F32),
            pltpu.VMEM((2048, 128), F32),
        ]
        + [pltpu.SemaphoreType.DMA] * 9
        + EVERYONE,
        compiler_params=pltpu.CompilerParams(
            collective_id=2, has_side_effects=True, vmem_limit_bytes=VMEM_LIMIT
        ),
        cost_estimate=cost(38),
        name="triangle",
    )(mask, cols, mix, output, left, right, gate_w, out_w)


def shards(
    pair_rep,
    tile_mask,
    chain_ids,
    chain_bias,
    row_project,
    row_bias_proj,
    row_output,
    col_project,
    col_bias_proj,
    col_output,
    tri_left,
    tri_right,
    tri_gate,
    tri_output,
):
    ids = chain_ids.reshape(1, 512)
    row_w, col_w = row_bias_proj.T, col_bias_proj.T
    mask, add = tile_mask, chain_bias
    g, *projected, steps = start(pair_rep, row_w, row_project)
    mix = attention(0, mask, add, g, ids, steps, projected)
    g, *projected, steps, cols = middle(pair_rep, mix, row_output, col_w, col_project)
    mix = attention(1, mask, add, g, ids, steps, projected)
    return triangle(mask, cols, mix, col_output, tri_left, tri_right, tri_gate, tri_output)


def solution(mesh):
    spec = P(("row", "col"), None, None)
    return jax.shard_map(
        shards,
        mesh=mesh,
        in_specs=(spec,) + (P(),) * 13,
        out_specs=P("row", "col", None),
        check_vma=False,
    )
```
